256 devices in a mesh: lon: 16 (over z, y_hi), lat: 16 (over x, y_lo, core).
Axes of the slice: x: 4, y: 4 (y_hi: 2, y_lo: 2; y = y_hi * 2 + y_lo), z: 8, core: 2. Of those that a mesh axis runs over, the one named last changes fastest.
Arguments:
- grid: bfloat16 [8, 96, 192, 192], P(None, 'lat', 'lon'), may hold values from -24 to 24
- gains: float32 [2, 2, 192], replicated, may hold values from 0.1 to 1.9
- w_qkv: bfloat16 [2, 192, 576], replicated, may hold values from -1 to 1
- w_proj: bfloat16 [2, 192, 192], replicated, may hold values from -0.4375 to 0.4375
- w_up: bfloat16 [2, 192, 768], replicated, may hold values from -0.4375 to 0.4375
- w_down: bfloat16 [2, 768, 192], replicated, may hold values from -0.21875 to 0.21875
- tables: float32 [2, 4, 16, 6, 3312], P(None, None, 'lat'), may hold values from -4 to 4
Outputs:
- result: bfloat16 [8, 96, 192, 192], P(None, 'lat', 'lon')
The draws below stay inside these ranges and needn't reach their ends.
All inputs are finite; a program needn't handle non-finite values.
Results may differ from the reference program's by a relative error of at most 0.02.
Values may be sent and summed in bfloat16 or wider, within the bound.
No kernel may reach another device: no remote copies, remote signals or barrier semaphores. Data moves between devices by JAX's collectives and lax.ppermute only.
A program may use at most 128 MiB of HBM per device.

```python
import jax
import jax.numpy as jnp
from jax import lax

C = 192
HEADS = 6
FF = 768
Z = 8
WZ = 2
WLAT = 6
WLON = 12
LAYERS = 2
NREL = 3312
LAT = 96
LON = 192


def draw_grid(key, part):
    key = jax.random.fold_in(key, 11)
    keys = jax.random.split(key, 1)
    base = jax.random.normal(keys[0], (Z, LAT, LON, C), jnp.float32)
    return jnp.clip(base, -6.0, 6.0).astype(jnp.bfloat16)


def draw_w_qkv(key, part):
    key = jax.random.fold_in(key, 23)
    keys = jax.random.split(key, 3)
    base = jax.random.normal(keys[2], (LAYERS, C, 3 * C), jnp.float32) * C ** (-0.5)
    return jnp.clip(base, -1.0, 1.0).astype(jnp.bfloat16)


def shard_levels(rng, shape, shards, smallest, high):
    factor_of, own = 1.0, jax.random.fold_in(rng, 6)
    for axis_at, blocks in shards:
        steps = jnp.exp(jax.random.uniform(jax.random.fold_in(own, axis_at), (blocks,), jnp.float32, smallest / len(shards), high / len(shards)))
        factor_of = factor_of * jnp.repeat(steps, shape[axis_at] // blocks).reshape([-1 if axis == axis_at else 1 for axis in range(len(shape))])
    return factor_of


def gaussian(own_key, shape, scale, most, cuts=(), held_as=jnp.bfloat16):
    drawn = scale * jax.random.normal(own_key, shape, jnp.float32)
    if cuts:
        drawn = drawn * shard_levels(own_key, shape, cuts, -0.22, 0.18)
    return jnp.clip(drawn, -most, most).astype(held_as)


def setup_inputs(seed: int = 0) -> dict:
    arg_keys = jax.random.split(jax.random.key(seed), 8)
    return {
        "grid": draw_grid(jax.random.fold_in(arg_keys[7], 71), 0),
        "gains": jnp.clip(1.0 + 0.18 * jax.random.normal(arg_keys[1], (LAYERS, 2, C), jnp.float32), 0.1, 1.9),
        "w_qkv": draw_w_qkv(jax.random.fold_in(arg_keys[7], 71), 0),
        "w_proj": gaussian(arg_keys[3], (LAYERS, C, C), C ** -0.5, 0.4375),
        "w_up": gaussian(arg_keys[4], (LAYERS, C, FF), C ** -0.5, 0.4375),
        "w_down": gaussian(arg_keys[5], (LAYERS, FF, C), FF ** -0.5, 0.21875),
        "tables": gaussian(arg_keys[6], (LAYERS, Z // WZ, LAT // WLAT, HEADS, NREL), 1.0, 4.0, ((2, 16),), jnp.float32),
    }


EPS = 1e-05

def toeplitz_table():
    band = jnp.arange(2 * WLON - 1, dtype=jnp.int32)[:, None, None]
    rows_at = jnp.arange(WLON, dtype=jnp.int32)[None, :, None]
    cols_at = jnp.arange(WLON, dtype=jnp.int32)[None, None, :]
    return (cols_at - rows_at + WLON - 1 == band).astype(jnp.float32)

def expand_bias(table):
    zwin, rwin = (table.shape[0], table.shape[1])
    shaped = table.reshape(zwin, rwin, HEADS, WZ, WZ, WLAT, WLAT, 2 * WLON - 1)
    full = jnp.einsum('zrhijmnd,dab->zrhimajnb', shaped, toeplitz_table(), precision=lax.Precision.HIGHEST)
    span = WZ * WLAT * WLON
    return full.reshape(zwin, rwin, HEADS, span, span)

def region_mask(level_ids, row_ids):
    levels = level_ids.reshape(-1, WZ)
    lats = row_ids.reshape(-1, WLAT)
    code = levels[:, None, :, None, None] * 2 + lats[None, :, None, :, None] + jnp.zeros((WLON,), jnp.int32)
    code = code.reshape(levels.shape[0], lats.shape[0], WZ * WLAT * WLON)
    return code[..., :, None] == code[..., None, :]

def to_windows(grid):
    depth, rows, cols, chan = grid.shape
    split = grid.reshape(depth // WZ, WZ, rows // WLAT, WLAT, cols // WLON, WLON, chan)
    split = split.transpose(0, 2, 4, 1, 3, 5, 6)
    return split.reshape(depth // WZ, rows // WLAT, cols // WLON, WZ * WLAT * WLON, chan)

def from_windows(tiles, depth, rows, cols):
    chan = tiles.shape[-1]
    split = tiles.reshape(depth // WZ, rows // WLAT, cols // WLON, WZ, WLAT, WLON, chan)
    return split.transpose(0, 3, 1, 4, 2, 5, 6).reshape(depth, rows, cols, chan)

def normalize(values, gain):
    mean = lax.optimization_barrier(jnp.mean(values, axis=-1, keepdims=True))
    centered = values - mean
    var = lax.optimization_barrier(jnp.mean(centered * centered, axis=-1, keepdims=True))
    return (centered * lax.rsqrt(var + EPS) * gain).astype(jnp.bfloat16)

def window_block(grid, gain_one, w_qkv, w_proj, gain_two, w_up, w_down, table, allowed):
    depth, rows, cols, chan = grid.shape
    tiles = to_windows(grid)
    zwin, rwin, lwin, span, _ = tiles.shape
    resid = tiles.astype(jnp.float32).reshape(-1, chan)
    normed = normalize(resid, gain_one)
    qkv = jnp.dot(normed, w_qkv, preferred_element_type=jnp.float32).astype(jnp.bfloat16)
    qkv = qkv.reshape(zwin, rwin, lwin, span, 3, HEADS, chan // HEADS)
    query = qkv[:, :, :, :, 0].astype(jnp.float32)
    keys = qkv[:, :, :, :, 1].astype(jnp.float32)
    values = qkv[:, :, :, :, 2].astype(jnp.float32)
    scale = (chan // HEADS) ** (-0.5)
    scores = jnp.einsum('zrlqhd,zrlkhd->zrlhqk', query, keys) * scale
    scores = scores + expand_bias(table)[:, :, None]
    if allowed is not None:
        scores = jnp.where(allowed[:, :, None, None], scores, -1000000000.0)
    top = lax.optimization_barrier(jnp.max(scores, axis=-1, keepdims=True))
    weights = jnp.exp(scores - top)
    probs = (weights / lax.optimization_barrier(jnp.sum(weights, axis=-1, keepdims=True))).astype(jnp.bfloat16)
    mixed = jnp.einsum('zrlhqk,zrlkhd->zrlqhd', probs.astype(jnp.float32), values).astype(jnp.bfloat16)
    attn = jnp.dot(mixed.reshape(-1, chan), w_proj, preferred_element_type=jnp.float32)
    first = (resid + attn).astype(jnp.bfloat16)
    inner = normalize(first.astype(jnp.float32), gain_two)
    hidden = jax.nn.gelu(jnp.dot(inner, w_up, preferred_element_type=jnp.float32), approximate=False).astype(jnp.bfloat16)
    out = (first.astype(jnp.float32) + jnp.dot(hidden, w_down, preferred_element_type=jnp.float32)).astype(jnp.bfloat16)
    return from_windows(out.reshape(zwin, rwin, lwin, span, chan), depth, rows, cols)

def reference(grid, gains, w_qkv, w_proj, w_up, w_down, tables):
    level_ids = (jnp.arange(Z, dtype=jnp.int32) == Z - 1).astype(jnp.int32)
    current = grid
    for layer in range(LAYERS):
        shifted = layer % 2 == 1
        if shifted:
            current = jnp.roll(current, (-(WZ // 2), -(WLAT // 2), -(WLON // 2)), (0, 1, 2))
        source = current

        def one_row(index, source=source, layer=layer, shifted=shifted):
            slab = lax.dynamic_slice_in_dim(source, (index * WLAT).astype(jnp.int32), WLAT, 1)
            table = lax.dynamic_slice_in_dim(tables[layer], index.astype(jnp.int32), 1, 1)
            allowed = None
            if shifted:
                lat_rows = index * WLAT + jnp.arange(WLAT, dtype=jnp.int32)
                allowed = region_mask(level_ids, (lat_rows >= LAT - WLAT // 2).astype(jnp.int32))
            return window_block(slab, gains[layer, 0], w_qkv[layer], w_proj[layer], gains[layer, 1], w_up[layer], w_down[layer], table, allowed)
        slabs = lax.map(one_row, jnp.arange(LAT // WLAT, dtype=jnp.int32))
        current = slabs.transpose(1, 0, 2, 3, 4).reshape(Z, LAT, LON, C)
        if shifted:
            current = jnp.roll(current, (WZ // 2, WLAT // 2, WLON // 2), (0, 1, 2))
    return current
```

```python
import functools
import math

import jax
import jax.numpy as jnp
import ml_dtypes
import numpy as np
from jax import lax
from jax.experimental import pallas as pl
from jax.experimental.pallas import tpu as pltpu
from jax.sharding import PartitionSpec as P

C = 192
HEADS = 6
HEAD = 32
FF = 768
Z = 8
WZ = 2
WLAT = 6
WLON = 12
HLAT = 3
HLON = 6
SPAN = WZ * WLAT * WLON
QB = WZ * HLAT * HLON
QUAD = Z * HLAT * HLON
BAND = 2 * WLON - 1
TROW = WLAT * BAND
TW = 384
TILES = TW // 128
QL = HEADS * QB
PEN = 300

EPS = 1e-05
LOG2E = math.log2(math.e)
BIG = -1e30
F32 = jnp.float32
BF16 = jnp.bfloat16
NT = (((1,), (1,)), ((), ()))


def key_select(masked):
    sel = np.zeros((SPAN, TW), np.float32)
    for part_a in range(2):
        for part_b in range(2):
            for zj in range(WZ):
                for r in range(HLAT):
                    for o in range(HLON):
                        row = (part_a * 2 + part_b) * QB + zj * 18 + r * 6 + o
                        rj = part_a * HLAT + r
                        oj = part_b * HLON + o
                        sel[row, zj * TROW + rj * BAND + oj + WLON - 1] = 1
                        if masked:
                            sel[row, PEN + zj] = 1
                            sel[row, PEN + 2 + part_a] = 1
    return sel.astype(ml_dtypes.bfloat16)


def fold_matrix():
    fold = np.zeros((40, QL), np.float32)
    for lane in range(QL):
        fold[lane % QB, lane] = 1
    return fold.astype(ml_dtypes.bfloat16)


def head_mask():
    rows = np.arange(C)[:, None] // HEAD
    lanes = np.arange(QL)[None, :] // QB
    return (rows == lanes).astype(np.float32)


def normalize(values, gain):
    mean = jnp.mean(values, axis=-1, keepdims=True)
    centered = values - mean
    var = jnp.mean(centered * centered, axis=-1, keepdims=True)
    return (centered * lax.rsqrt(var + EPS) * gain).astype(BF16)


def dot(a, b):
    return jnp.dot(a, b, preferred_element_type=F32)


def dot_nt(a, b):
    return lax.dot_general(a, b, NT, preferred_element_type=F32)


def table_rows(table, base, half, rows_ref):
    blank = jnp.zeros((HEADS, TW - 2 * TROW), F32)
    for zi in range(WZ):
        for r in range(HLAT):
            at = [((zi * WZ + zj) * WLAT + half * HLAT + r) * TROW for zj in range(WZ)]
            wide = jnp.concatenate([table[:, k : k + TROW] for k in at] + [blank], axis=1)
            for t in range(TILES):
                rows_ref[t, pl.ds(base + zi * HLAT + r, HEADS, stride=6), :] = (
                    wide[:, t * 128 : (t + 1) * 128]
                )


def joined(tiles):
    return jnp.concatenate([tiles[t] for t in range(TILES)], axis=-1)


def expand_rows(rows, first, chunk, wide_ref):
    for o in range(HLON):
        shift = first + o
        rolled = pltpu.roll(rows, shift, 1) if shift else rows
        for t in range(TILES):
            wide_ref[chunk, t, pl.ds(o, QB, stride=6), :] = rolled[:QB, t * 128 : (t + 1) * 128]


def attend(keys, values_t, query, wide, select, fold, hmask, stack_ref):
    lanes = lax.broadcasted_iota(jnp.int32, (1, C), 1)
    for h in range(HEADS):
        own = (lanes >= h * HEAD) & (lanes < (h + 1) * HEAD)
        stack_ref[h * QB : (h + 1) * QB, :] = jnp.where(own, query, 0.0)
    scores = dot_nt(keys, stack_ref[...].astype(BF16)) + dot_nt(select, wide)
    top = jnp.max(scores, axis=0, keepdims=True)
    weights = jnp.exp2(scores - top)
    total = jnp.sum(weights, axis=0, keepdims=True)
    mixed = dot(values_t, weights.astype(BF16))
    mixed = (mixed * (hmask * (1.0 / total))).astype(BF16)
    return dot_nt(fold, mixed)[:QB]


def feed_forward(resid, mixed, gain_two, w_proj, w_up, w_down):
    first = (resid + dot(mixed, w_proj)).astype(BF16)
    first32 = first.astype(F32)
    inner = normalize(first32, gain_two)
    hidden = dot(inner, w_up)
    hidden = (hidden * 0.5 * (1.0 + lax.erf(hidden * (0.5**0.5)))).astype(BF16)
    return first32 + dot(hidden, w_down)


QSCALE = HEAD**-0.5 * LOG2E


def first_kernel(
    x_ref, gains_ref, wqkv_ref, wproj_ref, wup_ref, wdown_ref, tab_ref, tab1_ref,
    select_ref, fold_ref, hmask_ref,
    left_ref, right_ref, tabhi_ref,
    tok_ref, q_ref, o_ref, rows_ref, hi_ref, wide_ref, stack_ref, quad_ref,
):
    for z in range(Z):
        for r in range(WLAT):
            row = x_ref[z, r].astype(F32)
            base = (z // 2) * SPAN + (r // HLAT) * 2 * QB + (z % 2) * 18 + (r % HLAT) * 6
            tok_ref[base : base + 6, :] = row[:6]
            tok_ref[base + QB : base + QB + 6, :] = row[6:]
    hi_ref[...] = jnp.zeros_like(hi_ref)
    rows_ref[...] = jnp.zeros_like(rows_ref)
    for w in range(4):
        table_rows(tab1_ref[0, w, 0] * LOG2E, w * QB, 1, hi_ref)
    hi = joined(hi_ref).astype(BF16)
    tabhi_ref[0] = hi[:, :C]
    tabhi_ref[1] = hi[:, C:]
    gain_one = gains_ref[0, 0:1]
    gain_two = gains_ref[0, 1:2]
    wqk = wqkv_ref[0, :, : 2 * C]
    wv_t = wqkv_ref[0, :, 2 * C :].T
    select = select_ref[...]
    fold = fold_ref[...]
    hmask = hmask_ref[...]
    for w in range(4):
        table = tab_ref[0, w, 0] * LOG2E
        normed = normalize(tok_ref[w * SPAN : (w + 1) * SPAN, :], gain_one)
        both = dot(normed, wqk)
        q_ref[...] = both[:, :C] * QSCALE
        keys = both[:, C:].astype(BF16)
        values_t = dot_nt(wv_t, normed).astype(BF16)
        for a in range(2):
            table_rows(table, 0, a, rows_ref)
            rows = joined(rows_ref)
            for b in range(2):
                block = a * 2 + b
                chunk = w * 4 + block
                expand_rows(rows, b * HLON, block, wide_ref)
                o_ref[chunk * QB : (chunk + 1) * QB, :] = attend(
                    keys, values_t, q_ref[block * QB : (block + 1) * QB, :],
                    joined(wide_ref.at[block]).astype(BF16), select, fold, hmask, stack_ref,
                )
    tok_ref[...] = feed_forward(
        tok_ref[...], o_ref[...].astype(BF16), gain_two, wproj_ref[0], wup_ref[0], wdown_ref[0]
    )
    for b, out_ref in ((0, left_ref), (1, right_ref)):
        for a in range(2):
            for z in range(Z):
                base = (z // 2) * SPAN + (a * 2 + b) * QB + (z % 2) * 18
                to = (z + Z - 1) % Z * 18
                quad_ref[to : to + 18, :] = tok_ref[base : base + 18, :]
            out_ref[a] = quad_ref[...].astype(BF16)


def second_kernel(
    flags_ref, left_ref, right_ref, fl_ref, fr_ref, prev_ref, next_ref,
    gains_ref, wqkv_ref, wproj_ref, wup_ref, wdown_ref, tab_ref,
    select_ref, fold_ref, hmask_ref,
    out_ref,
    own_ref, xw_ref, q_ref, o_ref, rows_ref, wide_ref, stack_ref, quad_ref, nat_ref,
):
    gain_one = gains_ref[1, 0:1]
    gain_two = gains_ref[1, 1:2]
    wq = wqkv_ref[0, :, :C]
    wk = wqkv_ref[0, :, C : 2 * C]
    wv_t = wqkv_ref[0, :, 2 * C :].T
    select = select_ref[...]
    fold = fold_ref[...]
    hmask = hmask_ref[...]
    for b, ref in ((0, left_ref), (1, right_ref)):
        for a in range(2):
            at = (b * 2 + a) * QUAD
            own_ref[at : at + QUAD, :] = ref[a].astype(F32)
    q_ref[...] = dot(normalize(own_ref[...], gain_one), wq) * QSCALE
    lane = lax.broadcasted_iota(jnp.int32, (QL, 128), 1) + 256
    zi = (lax.broadcasted_iota(jnp.int32, (QL, 1), 0) % QB) // 18
    pen_z = jnp.where(((lane == PEN) & (zi == 1)) | ((lane == PEN + 1) & (zi == 0)), BIG, 0.0)
    first_rows = flags_ref[0]
    last_rows = flags_ref[1]
    lane_row = lane[:1]
    pen_prev = jnp.where((lane_row == PEN + 2) & (first_rows == 1), BIG, 0.0)
    pen_own = jnp.where((lane_row == PEN + 3) & (last_rows == 1), BIG, 0.0)
    rows_ref[...] = jnp.zeros_like(rows_ref)
    quad_ref[...] = prev_ref[4].astype(F32)
    nat_ref[:QUAD, :] = prev_ref[5].astype(F32)
    for zw in range(4):
        for a in range(2):
            if a == 0:
                part = slice(zw * QB, (zw + 1) * QB)
                rows = jnp.concatenate([quad_ref[part, :], nat_ref[part, :]], axis=1)
            else:
                table_rows(tab_ref[0, zw, 0] * LOG2E, 0, 0, rows_ref)
                rows = joined(rows_ref)[:QB]
            for b in range(2):
                chunk = (b * 2 + a) * 4 + zw
                expand_rows(rows, (1 - b) * HLON, chunk, wide_ref)
                tail = wide_ref[chunk, 2] + (pen_prev if a == 0 else pen_own)
                if zw == 3:
                    tail = tail + pen_z
                wide_ref[chunk, 2] = tail
    for a in range(2):
        for part_a in range(2):
            away = part_a == a
            if not away:
                cols = [fl_ref.at[a], left_ref.at[a], right_ref.at[a], fr_ref.at[a]]
            else:
                src = prev_ref if a == 0 else next_ref
                cols = [src.at[2], src.at[0], src.at[1], src.at[3]]
            for b in range(2):
                for part_b in range(2):
                    quad_ref[...] = cols[b * 2 + part_b][...].astype(F32)
                    at = (part_a * 2 + part_b) * QB
                    for zw in range(4):
                        chunk = (b * 2 + a) * 4 + zw
                        xw_ref[chunk, at : at + QB, :] = quad_ref[zw * QB : (zw + 1) * QB, :]
    for chunk in range(16):
        normed = normalize(xw_ref[chunk], gain_one)
        keys = dot(normed, wk).astype(BF16)
        values_t = dot_nt(wv_t, normed).astype(BF16)
        o_ref[chunk * QB : (chunk + 1) * QB, :] = attend(
            keys, values_t, q_ref[chunk * QB : (chunk + 1) * QB, :],
            joined(wide_ref.at[chunk]).astype(BF16), select, fold, hmask, stack_ref,
        )
    own_ref[...] = feed_forward(
        own_ref[...], o_ref[...].astype(BF16), gain_two, wproj_ref[0], wup_ref[0], wdown_ref[0]
    )
    for b in range(2):
        for z in range(Z):
            for r in range(WLAT):
                rolled = (z + Z - 1) % Z
                base = (b * 2 + r // HLAT) * QUAD + rolled * 18 + (r % HLAT) * 6
                at = (z * WLAT + r) * 16 + b * HLON
                nat_ref[at : at + HLON, :] = own_ref[base : base + HLON, :]
    for z in range(Z):
        for r in range(WLAT):
            at = (z * WLAT + r) * 16
            out_ref[z, r] = nat_ref[at : at + WLON, :].astype(BF16)


def whole(shape):
    return pl.BlockSpec(shape, lambda *_: (0,) * len(shape))


def picked(shape, layer):
    return pl.BlockSpec((1,) + shape[1:], lambda *_: (layer,) + (0,) * (len(shape) - 1))


def weight_specs(layer, gains, w_qkv, w_proj, w_up, w_down):
    return [whole(gains.shape)] + [picked(w.shape, layer) for w in (w_qkv, w_proj, w_up, w_down)]


PARAMS = pltpu.CompilerParams(vmem_limit_bytes=56 * 1024 * 1024)


def shifted(value, axis, steps):
    count = lax.axis_size(axis)
    pairs = [(source, (source + steps) % count) for source in range(count)]
    return lax.ppermute(value, axis, pairs)


def shards(grid, gains, w_qkv, w_proj, w_up, w_down, tables):
    plain = jnp.asarray(key_select(False))
    masked = jnp.asarray(key_select(True))
    fold = jnp.asarray(fold_matrix())
    hmask = jnp.asarray(head_mask())
    weights = (gains, w_qkv, w_proj, w_up, w_down)
    half = jax.ShapeDtypeStruct((2, QUAD, C), BF16)
    left, right, tabhi = pl.pallas_call(
        first_kernel,
        grid=(1,),
        in_specs=[whole(grid.shape)]
        + weight_specs(0, *weights)
        + [picked(tables.shape, 0), picked(tables.shape, 1)]
        + [whole(plain.shape), whole(fold.shape), whole(hmask.shape)],
        out_specs=[whole(half.shape)] * 3,
        out_shape=[half, half, half],
        scratch_shapes=[
            pltpu.VMEM((4 * SPAN, C), F32),
            pltpu.VMEM((SPAN, C), F32),
            pltpu.VMEM((4 * SPAN, C), F32),
            pltpu.VMEM((TILES, 40, 128), F32),
            pltpu.VMEM((TILES, 4 * QB, 128), F32),
            pltpu.VMEM((4, TILES, QL, 128), F32),
            pltpu.VMEM((QL, C), F32),
            pltpu.VMEM((QUAD, C), F32),
        ],
        compiler_params=PARAMS,
        name="first_layer",
    )(grid, *weights, tables, tables, plain, fold, hmask)
    from_left = shifted(right, "lon", 1)
    from_right = shifted(left, "lon", -1)
    down = jnp.concatenate([left[1:], right[1:], from_left[1:], from_right[1:], tabhi])
    up = jnp.concatenate([left[:1], right[:1], from_left[:1], from_right[:1]])
    from_prev = shifted(down, "lat", 1)
    from_next = shifted(up, "lat", -1)
    lat = lax.axis_index("lat")
    flags = jnp.stack([lat == 0, lat == lax.axis_size("lat") - 1]).astype(jnp.int32)
    moved = (left, right, from_left, from_right, from_prev, from_next)
    return pl.pallas_call(
        second_kernel,
        grid=(1,),
        in_specs=[pl.BlockSpec(memory_space=pltpu.SMEM)]
        + [whole(m.shape) for m in moved]
        + weight_specs(1, *weights)
        + [picked(tables.shape, 1)]
        + [whole(masked.shape), whole(fold.shape), whole(hmask.shape)],
        out_specs=whole(grid.shape),
        out_shape=jax.ShapeDtypeStruct(grid.shape, BF16),
        scratch_shapes=[
            pltpu.VMEM((4 * QUAD, C), F32),
            pltpu.VMEM((16, SPAN, C), F32),
            pltpu.VMEM((4 * QUAD, C), F32),
            pltpu.VMEM((4 * QUAD, C), F32),
            pltpu.VMEM((TILES, 40, 128), F32),
            pltpu.VMEM((16, TILES, QL, 128), F32),
            pltpu.VMEM((QL, C), F32),
            pltpu.VMEM((QUAD, C), F32),
            pltpu.VMEM((Z * WLAT * 16, C), F32),
        ],
        compiler_params=PARAMS,
        name="second_layer",
    )(flags, *moved, *weights, tables, masked, fold, hmask)


def solution(mesh):
    in_specs = (
        P(None, "lat", "lon", None),
        P(),
        P(),
        P(),
        P(),
        P(),
        P(None, None, "lat", None, None),
    )
    out_specs = P(None, "lat", "lon", None)
    return jax.shard_map(shards, mesh=mesh, in_specs=in_specs, out_specs=out_specs, check_vma=False)
```

```python
import functools
import math

import jax
import jax.numpy as jnp
import ml_dtypes
import numpy as np
from jax import lax
from jax.experimental import pallas as pl
from jax.experimental.pallas import tpu as pltpu
from jax.sharding import PartitionSpec as P

C = 192
HEADS = 6
HEAD = 32
FF = 768
Z = 8
WZ = 2
WLAT = 6
WLON = 12
HLAT = 3
HLON = 6
SPAN = WZ * WLAT * WLON
QB = WZ * HLAT * HLON
QUAD = Z * HLAT * HLON
BAND = 2 * WLON - 1
TROW = WLAT * BAND
TW = 384
TILES = TW // 128
QP = 40
SP = 4 * QP
QL = HEADS * QP
PEN = 300
ONE = 330
TSPAN = 168

EPS = 1e-05
LOG2E = math.log2(math.e)
BIG = -1e30
F32 = jnp.float32
BF16 = jnp.bfloat16
NT = (((1,), (1,)), ((), ()))


def key_select(masked):
    sel = np.zeros((TW, SP), np.float32)
    for part in range(4):
        for zj in range(WZ):
            for r in range(HLAT):
                for o in range(HLON):
                    col = part * QP + zj * 18 + r * 6 + o
                    rj = part // 2 * HLAT + r
                    oj = part % 2 * HLON + o
                    sel[zj * TROW + rj * BAND + oj + WLON - 1, col] = 1
                    if masked:
                        sel[PEN + zj, col] = 1
                        sel[PEN + 2 + part // 2, col] = 1
        sel[ONE : ONE + WLON, part * QP + QB : (part + 1) * QP] = BIG
    return sel.astype(ml_dtypes.bfloat16)


def normalize(values, gain):
    mean = jnp.mean(values, axis=-1, keepdims=True)
    centered = values - mean
    var = jnp.mean(centered * centered, axis=-1, keepdims=True)
    return (centered * lax.rsqrt(var + EPS) * gain).astype(BF16)


def dot(a, b):
    return jnp.dot(a, b, preferred_element_type=F32)


def dot_nt(a, b):
    return lax.dot_general(a, b, NT, preferred_element_type=F32)


def table_rows(table, base, half, stride, rows_ref):
    blank = jnp.zeros((HEADS, TW - 2 * TROW), F32)
    lane = lax.broadcasted_iota(jnp.int32, blank.shape, 1) + 2 * TROW
    blank = jnp.where(lane == ONE, 1.0, blank)
    for zi in range(WZ):
        for r in range(HLAT):
            at = [((zi * WZ + zj) * WLAT + half * HLAT + r) * TROW for zj in range(WZ)]
            wide = jnp.concatenate([table[:, k : k + TROW] for k in at] + [blank], axis=1)
            for t in range(TILES):
                rows_ref[t, pl.ds(base + zi * HLAT + r, HEADS, stride=stride), :] = (
                    wide[:, t * 128 : (t + 1) * 128]
                )


def joined(tiles):
    return jnp.concatenate([tiles[t] for t in range(TILES)], axis=-1)


def expand_rows(rows, first, chunk, wide_ref):
    for o in range(HLON):
        shift = first + o
        rolled = pltpu.roll(rows, shift, 1) if shift else rows
        for h in range(HEADS):
            for t in range(TILES):
                wide_ref[chunk, t, pl.ds(h * QP + o, 6, stride=6), :] = (
                    rolled[h * 8 : h * 8 + 6, t * 128 : (t + 1) * 128]
                )


def attend(items, select):
    lanes = lax.broadcasted_iota(jnp.int32, (1, C), 1)
    own = [(lanes >= h * HEAD) & (lanes < (h + 1) * HEAD) for h in range(HEADS)]
    stacks = [
        jnp.concatenate([jnp.where(own[h], q, 0.0) for h in range(HEADS)], axis=0).astype(BF16)
        for _, _, q, _ in items
    ]
    scores = [dot_nt(st, it[0]) + dot(it[3], select) for st, it in zip(stacks, items)]
    weights = [
        jnp.exp2(s - jnp.max(s, axis=1, keepdims=True)).astype(BF16) for s in scores
    ]
    mixed = [dot(p, it[1]) for p, it in zip(weights, items)]
    outs = []
    for m in mixed:
        scaled = m[:, :C] * (1.0 / m[:, C : C + 1])
        out = jnp.where(own[0], scaled[:QP], 0.0)
        for h in range(1, HEADS):
            out = jnp.where(own[h], scaled[h * QP : (h + 1) * QP], out)
        outs.append(out)
    return outs


def feed_forward(resid, mixed, gain_two, w_proj, w_up, w_down_t):
    first = (resid + dot(mixed, w_proj)).astype(BF16)
    first32 = first.astype(F32)
    inner = normalize(first32, gain_two)
    hidden = dot(inner, w_up)
    hidden = (hidden * 0.5 * (1.0 + lax.erf(hidden * (0.5**0.5)))).astype(BF16)
    return first32 + dot_nt(hidden, w_down_t)


QSCALE = HEAD**-0.5 * LOG2E


def with_ones(values):
    lanes = lax.broadcasted_iota(jnp.int32, values.shape, 1)
    return jnp.where(lanes == C, 1.0, values).astype(BF16)


def value_weights(wqkv_ref):
    return jnp.concatenate([wqkv_ref[0, :, 2 * C :], jnp.zeros((C, 256 - C), BF16)], axis=1)


def tiles_of(value):
    return value[:, :128], jnp.concatenate([value[:, 128:], value[:, 128:]], axis=1)


def whole_row(first, second):
    return jnp.concatenate([first, second[:, : C - 128]], axis=1)


def first_kernel(
    x_ref, gains_ref, wqkv_ref, wproj_ref, wup_ref, wdown_ref, tab_ref, tab1_ref,
    select_ref,
    left_ref, right_ref, tabhi_ref,
    plain_ref, tok_ref, o_ref, rows_ref, hi_ref, wide_ref,
):
    plain_ref[...] = jnp.zeros_like(plain_ref)
    for r in range(WLAT):
        for o in range(WLON):
            part = r // HLAT * 2 + o // HLON
            at = (r % HLAT) * 6 + o % HLON
            for t, tile in enumerate(tiles_of(x_ref[r, o].astype(F32))):
                plain_ref[part, t, pl.ds(at, Z, stride=18), :] = tile
    for part in range(4):
        for w in range(4):
            rows = pl.ds(w * QB, QP)
            at = (part * 4 + w) * QP
            tok_ref[at : at + QP, :] = whole_row(plain_ref[part, 0, rows, :], plain_ref[part, 1, rows, :])
    for w in range(4):
        table_rows(tab1_ref[0, w, 0] * LOG2E, w * QP, 1, 6, hi_ref)
    hi = joined(hi_ref).astype(BF16)
    for w in range(4):
        tabhi_ref[0, w] = joined(hi_ref.at[:, pl.ds(w * QP, QP)])[:, :C].astype(BF16)
        tabhi_ref[1, w] = joined(hi_ref.at[:, pl.ds(w * QP, QP)])[:, C:].astype(BF16)
    gain_one = gains_ref[0, 0:1]
    gain_two = gains_ref[0, 1:2]
    wqk = wqkv_ref[0, :, : 2 * C]
    wv = value_weights(wqkv_ref)
    select = select_ref[...]
    for w in range(4):
        table = tab_ref[0, w, 0] * LOG2E
        for a in range(2):
            table_rows(table, 0, a, 8, rows_ref.at[a])
            rows = joined(rows_ref.at[a])
            for b in range(2):
                expand_rows(rows, b * HLON, w * 4 + a * 2 + b, wide_ref)
    for w in range(4):
        tokens = jnp.concatenate(
            [tok_ref[(part * 4 + w) * QP : (part * 4 + w + 1) * QP, :] for part in range(4)], axis=0
        )
        normed = normalize(tokens, gain_one)
        both = dot(normed, wqk)
        query = both[:, :C] * QSCALE
        keys = both[:, C:].astype(BF16)
        values = with_ones(dot(normed, wv))
        items = [
            (keys, values, query[part * QP : (part + 1) * QP], joined(wide_ref.at[w * 4 + part]).astype(BF16))
            for part in range(4)
        ]
        for part, out in enumerate(attend(items, select)):
            o_ref[(part * 4 + w) * QP : (part * 4 + w + 1) * QP, :] = out
    tok_ref[...] = feed_forward(
        tok_ref[...], o_ref[...].astype(BF16), gain_two, wproj_ref[0], wup_ref[0], wdown_ref[0]
    )
    for b, out_ref in ((0, left_ref), (1, right_ref)):
        for a in range(2):
            part = a * 2 + b
            for w in range(4):
                at = (part * 4 + w) * QP
                for t, tile in enumerate(tiles_of(tok_ref[at : at + QB, :])):
                    plain_ref[part, t, pl.ds(w * QB, QB), :] = tile
                    if w == 0:
                        plain_ref[part, t, pl.ds(QUAD, 18), :] = tile[:18]
            for zw in range(4):
                rows = pl.ds(zw * QB + 18, QP)
                out_ref[a, zw] = whole_row(plain_ref[part, 0, rows, :], plain_ref[part, 1, rows, :]).astype(BF16)


def second_kernel(
    flags_ref, left_ref, right_ref, fl_ref, fr_ref, prev_ref, next_ref,
    gains_ref, wqkv_ref, wproj_ref, wup_ref, wdown_ref, tab_ref,
    select_ref,
    out_ref,
    plain_ref, own_ref, q_ref, o_ref, rows_ref, hi_ref, wide_ref,
):
    gain_one = gains_ref[1, 0:1]
    gain_two = gains_ref[1, 1:2]
    wq = wqkv_ref[0, :, :C]
    wk = wqkv_ref[0, :, C : 2 * C]
    wv = value_weights(wqkv_ref)
    select = select_ref[...]
    for b, ref in ((0, left_ref), (1, right_ref)):
        for a in range(2):
            for zw in range(4):
                at = ((b * 2 + a) * 4 + zw) * QP
                own_ref[at : at + QP, :] = ref[a, zw].astype(F32)
    q_ref[...] = dot(normalize(own_ref[...], gain_one), wq) * QSCALE
    lane = lax.broadcasted_iota(jnp.int32, (QL, 128), 1) + 256
    zi = (lax.broadcasted_iota(jnp.int32, (QL, 1), 0) % QP) // 18
    pen_z = jnp.where(((lane == PEN) & (zi == 1)) | ((lane == PEN + 1) & (zi == 0)), BIG, 0.0)
    lane_row = lane[:1]
    pen_prev = jnp.where((lane_row == PEN + 2) & (flags_ref[0] == 1), BIG, 0.0)
    pen_own = jnp.where((lane_row == PEN + 3) & (flags_ref[1] == 1), BIG, 0.0)
    for zw in range(4):
        table_rows(tab_ref[0, zw, 0] * LOG2E, 0, 0, 8, rows_ref.at[1])
        hi = jnp.concatenate([prev_ref[4, zw], prev_ref[5, zw]], axis=1).astype(F32)
        for t in range(TILES):
            hi_ref[t] = hi[:, t * 128 : (t + 1) * 128]
            for h in range(HEADS):
                rows_ref[0, t, h * 8 : h * 8 + 6, :] = hi_ref[t, h * 6 : h * 6 + 6, :]
        for a in range(2):
            rows = joined(rows_ref.at[a])
            for b in range(2):
                chunk = (b * 2 + a) * 4 + zw
                expand_rows(rows, (1 - b) * HLON, chunk, wide_ref)
                tail = wide_ref[chunk, 2] + (pen_prev if a == 0 else pen_own)
                if zw == 3:
                    tail = tail + pen_z
                wide_ref[chunk, 2] = tail
    above = [prev_ref.at[2], prev_ref.at[0], prev_ref.at[1], prev_ref.at[3]]
    here = [[fl_ref.at[a], left_ref.at[a], right_ref.at[a], fr_ref.at[a]] for a in range(2)]
    below = [next_ref.at[2], next_ref.at[0], next_ref.at[1], next_ref.at[3]]
    for b in range(2):
        for a in range(2):
            pair = (above, here[0]) if a == 0 else (here[1], below)
            sources = [pair[part // 2][b * 2 + part % 2] for part in range(4)]
            items = []
            for zw in range(4):
                chunk = (b * 2 + a) * 4 + zw
                tokens = jnp.concatenate([src[zw].astype(F32) for src in sources], axis=0)
                normed = normalize(tokens, gain_one)
                keys = dot(normed, wk).astype(BF16)
                values = with_ones(dot(normed, wv))
                items.append(
                    (keys, values, q_ref[chunk * QP : (chunk + 1) * QP, :], joined(wide_ref.at[chunk]).astype(BF16))
                )
            for zw, out in enumerate(attend(items, select)):
                chunk = (b * 2 + a) * 4 + zw
                o_ref[chunk * QP : (chunk + 1) * QP, :] = out
    own_ref[...] = feed_forward(
        own_ref[...], o_ref[...].astype(BF16), gain_two, wproj_ref[0], wup_ref[0], wdown_ref[0]
    )
    for part in range(4):
        a, b = divmod(part, 2)
        for zw in range(4):
            at = ((b * 2 + a) * 4 + zw) * QP
            for t, tile in enumerate(tiles_of(own_ref[at : at + QB, :])):
                if zw < 3:
                    plain_ref[part, t, pl.ds(zw * QB + 18, QB), :] = tile
                else:
                    plain_ref[part, t, pl.ds(zw * QB + 18, 18), :] = tile[:18]
                    plain_ref[part, t, pl.ds(0, 18), :] = tile[18:]
    for r in range(WLAT):
        for o in range(WLON):
            part = r // HLAT * 2 + o // HLON
            at = (r % HLAT) * 6 + o % HLON
            out_ref[r, o] = whole_row(
                plain_ref[part, 0, pl.ds(at, Z, stride=18), :], plain_ref[part, 1, pl.ds(at, Z, stride=18), :]
            ).astype(BF16)


def whole(shape):
    return pl.BlockSpec(shape, lambda *_: (0,) * len(shape))


def picked(shape, layer):
    return pl.BlockSpec((1,) + shape[1:], lambda *_: (layer,) + (0,) * (len(shape) - 1))


def weight_specs(layer, gains, w_qkv, w_proj, w_up, w_down):
    return [whole(gains.shape)] + [picked(w.shape, layer) for w in (w_qkv, w_proj, w_up, w_down)]


PARAMS = pltpu.CompilerParams(vmem_limit_bytes=56 * 1024 * 1024)


def shifted(value, axis, steps):
    count = lax.axis_size(axis)
    pairs = [(source, (source + steps) % count) for source in range(count)]
    return lax.ppermute(value, axis, pairs)


def shards(grid, gains, w_qkv, w_proj, w_up, w_down, tables):
    grid = grid.transpose(1, 2, 0, 3)
    w_down = w_down.transpose(0, 2, 1)
    plain = jnp.asarray(key_select(False))
    masked = jnp.asarray(key_select(True))
    weights = (gains, w_qkv, w_proj, w_up, w_down)
    half = jax.ShapeDtypeStruct((2, 4, QP, C), BF16)
    tok = pltpu.VMEM((16 * QP, C), F32)
    plain_tok = pltpu.VMEM((4, 2, TSPAN, 128), F32)
    left, right, tabhi = pl.pallas_call(
        first_kernel,
        grid=(1,),
        in_specs=[whole(grid.shape)]
        + weight_specs(0, *weights)
        + [picked(tables.shape, 0), picked(tables.shape, 1)]
        + [whole(plain.shape)],
        out_specs=[whole(half.shape)] * 3,
        out_shape=[half, half, half],
        scratch_shapes=[
            plain_tok, tok, tok,
            pltpu.VMEM((2, TILES, 48, 128), F32),
            pltpu.VMEM((TILES, 4 * QP, 128), F32),
            pltpu.VMEM((16, TILES, QL, 128), F32),
        ],
        compiler_params=PARAMS,
        name="first_layer",
    )(grid, *weights, tables, tables, plain)
    from_left = shifted(right, "lon", 1)
    from_right = shifted(left, "lon", -1)
    down = jnp.concatenate([left[1:], right[1:], from_left[1:], from_right[1:], tabhi])
    up = jnp.concatenate([left[:1], right[:1], from_left[:1], from_right[:1]])
    from_prev = shifted(down, "lat", 1)
    from_next = shifted(up, "lat", -1)
    lat = lax.axis_index("lat")
    flags = jnp.stack([lat == 0, lat == lax.axis_size("lat") - 1]).astype(jnp.int32)
    moved = (left, right, from_left, from_right, from_prev, from_next)
    out = pl.pallas_call(
        second_kernel,
        grid=(1,),
        in_specs=[pl.BlockSpec(memory_space=pltpu.SMEM)]
        + [whole(m.shape) for m in moved]
        + weight_specs(1, *weights)
        + [picked(tables.shape, 1)]
        + [whole(masked.shape)],
        out_specs=whole(grid.shape),
        out_shape=jax.ShapeDtypeStruct(grid.shape, BF16),
        scratch_shapes=[
            plain_tok, tok, tok, tok,
            pltpu.VMEM((2, TILES, 48, 128), F32),
            pltpu.VMEM((TILES, QP, 128), F32),
            pltpu.VMEM((16, TILES, QL, 128), F32),
        ],
        compiler_params=PARAMS,
        name="second_layer",
    )(flags, *moved, *weights, tables, masked)
    return out.transpose(2, 0, 1, 3)


def solution(mesh):
    in_specs = (
        P(None, "lat", "lon", None),
        P(),
        P(),
        P(),
        P(),
        P(),
        P(None, None, "lat", None, None),
    )
    out_specs = P(None, "lat", "lon", None)
    return jax.shard_map(shards, mesh=mesh, in_specs=in_specs, out_specs=out_specs, check_vma=False)
```

```python
import functools
import math

import jax
import jax.numpy as jnp
import numpy as np
from jax import lax
from jax.experimental import pallas as pl
from jax.experimental.pallas import tpu as pltpu
from jax.sharding import PartitionSpec as P

C = 192
HEADS = 6
HEAD = 32
FF = 768
Z = 8
WZ = 2
WLAT = 6
WLON = 12
HLAT = 3
HLON = 6
SPAN = WZ * WLAT * WLON
QB = WZ * HLAT * HLON
QUAD = Z * HLAT * HLON
BAND = 2 * WLON - 1
TROW = WLAT * BAND
TW = 384
TILES = TW // 128
QP = 40
SP = 4 * QP
QL = HEADS * QP
PEN = 300
ONE = 330
TSPAN = 168

EPS = 1e-05
LOG2E = math.log2(math.e)
BIG = -1e30
F32 = jnp.float32
BF16 = jnp.bfloat16
NT = (((1,), (1,)), ((), ()))


def key_select(masked):
    sel = np.zeros((TW, SP), np.float32)
    for part in range(4):
        for zj in range(WZ):
            for r in range(HLAT):
                for o in range(HLON):
                    col = part * QP + zj * 18 + r * 6 + o
                    rj = part // 2 * HLAT + r
                    oj = part % 2 * HLON + o
                    sel[zj * TROW + rj * BAND + oj + WLON - 1, col] = 1
                    if masked:
                        sel[PEN + zj, col] = 1
                        sel[PEN + 2 + part // 2, col] = 1
        sel[ONE : ONE + WLON, part * QP + QB : (part + 1) * QP] = BIG
    return sel


def normalize(values, gain):
    mean = jnp.mean(values, axis=-1, keepdims=True)
    centered = values - mean
    var = jnp.mean(centered * centered, axis=-1, keepdims=True)
    return (centered * lax.rsqrt(var + EPS) * gain).astype(BF16)


def dot(a, b):
    return jnp.dot(a, b, preferred_element_type=F32)


def dot_nt(a, b):
    return lax.dot_general(a, b, NT, preferred_element_type=F32)


def table_rows(table, half, rows_ref):
    blank = jnp.zeros((HEADS, TW - 2 * TROW), F32)
    lane = lax.broadcasted_iota(jnp.int32, blank.shape, 1) + 2 * TROW
    blank = jnp.where(lane == ONE, 1.0, blank)
    for zi in range(WZ):
        for r in range(HLAT):
            at = [((zi * WZ + zj) * WLAT + half * HLAT + r) * TROW for zj in range(WZ)]
            wide = jnp.concatenate([table[:, k : k + TROW] for k in at] + [blank], axis=1)
            for t in range(TILES):
                rows_ref[t, pl.ds(zi * HLAT + r, HEADS, stride=8), :] = (
                    wide[:, t * 128 : (t + 1) * 128]
                )


def joined(tiles):
    return jnp.concatenate([tiles[t] for t in range(TILES)], axis=-1)


def expand_rows(rows, first, chunk, wide_ref):
    for o in range(HLON):
        shift = first + o
        rolled = pltpu.roll(rows, shift, 1) if shift else rows
        for h in range(HEADS):
            for t in range(TILES):
                wide_ref[chunk, t, pl.ds(h * QP + o, 6, stride=6), :] = (
                    rolled[h * 8 : h * 8 + 6, t * 128 : (t + 1) * 128]
                )


def head_lanes():
    lanes = lax.broadcasted_iota(jnp.int32, (1, C), 1)
    return [(lanes >= h * HEAD) & (lanes < (h + 1) * HEAD) for h in range(HEADS)]


def attend(items):
    own = head_lanes()
    stacks = [
        jnp.concatenate([jnp.where(own[h], q, 0.0) for h in range(HEADS)], axis=0).astype(BF16)
        for _, _, q, _ in items
    ]
    scores = [dot_nt(st, it[0]) + it[3]() for st, it in zip(stacks, items)]
    weights = [
        jnp.exp2(s - jnp.max(s, axis=1, keepdims=True)).astype(BF16) for s in scores
    ]
    mixed = [dot(p, it[1]) for p, it in zip(weights, items)]
    outs = []
    for m in mixed:
        scaled = m[:, :C] * (1.0 / m[:, C : C + 1])
        out = scaled[:QP]
        for h in range(1, HEADS):
            out = jnp.where(own[h], scaled[h * QP : (h + 1) * QP], out)
        outs.append(out)
    return outs


class Fetch:
    def __init__(self, sems):
        self.sems = sems
        self.copies = {}

    def start(self, name, source, target):
        copy = pltpu.make_async_copy(source, target, self.sems.at[len(self.copies)])
        self.copies[name] = copy
        copy.start()

    def wait(self, *names):
        for name in names:
            self.copies[name].wait()


def feed_forward(resid, mixed, gain_two, w_proj, w_up, w_down_t):
    first = (resid + dot(mixed, w_proj)).astype(BF16)
    first32 = first.astype(F32)
    inner = normalize(first32, gain_two)
    hidden = dot(inner, w_up)
    hidden = (hidden * 0.5 * (1.0 + lax.erf(hidden * (0.5**0.5)))).astype(BF16)
    return first32 + dot_nt(hidden, w_down_t)


QSCALE = HEAD**-0.5 * LOG2E


def with_ones(values):
    lanes = lax.broadcasted_iota(jnp.int32, values.shape, 1)
    return jnp.where(lanes == C, 1.0, values).astype(BF16)


def value_weights(qkv_ref):
    return jnp.concatenate([qkv_ref[:, 2 * C :], jnp.zeros((C, 256 - C), BF16)], axis=1)


def tiles_of(value):
    return value[:, :128], jnp.concatenate([value[:, 128:], value[:, 128:]], axis=1)


def whole_row(first, second):
    return jnp.concatenate([first, second[:, : C - 128]], axis=1)


def first_kernel(
    x_ref, gains_ref, wqkv_ref, wproj_ref, wup_ref, wdown_ref, tab_ref,
    select_ref,
    fast_ref, slow_ref,
    plain_ref, tok_ref, o_ref, rows_ref, wide_ref,
):
    plain_ref[...] = jnp.zeros_like(plain_ref)
    for r in range(WLAT):
        for o in range(WLON):
            part = r // HLAT * 2 + o // HLON
            at = (r % HLAT) * 6 + o % HLON
            for t, tile in enumerate(tiles_of(x_ref[r, o].astype(F32))):
                plain_ref[part, t, pl.ds(at, Z, stride=18), :] = tile
    for part in range(4):
        for w in range(4):
            rows = pl.ds(w * QB, QP)
            at = (part * 4 + w) * QP
            tok_ref[at : at + QP, :] = whole_row(plain_ref[part, 0, rows, :], plain_ref[part, 1, rows, :])
    select = select_ref[...].astype(BF16)
    for w in range(4):
        table = tab_ref[0, w, :, 0, :] * LOG2E
        for a in range(2):
            table_rows(table, a, rows_ref.at[a])
            rows = joined(rows_ref.at[a])
            for b in range(2):
                expand_rows(rows, b * HLON, w * 4 + a * 2 + b, wide_ref)
    gain_one = gains_ref[0, 0:1]
    gain_two = gains_ref[0, 1:2]
    wqk = wqkv_ref[0, :, : 2 * C]
    wv = value_weights(wqkv_ref.at[0])
    for w in range(4):
        tokens = jnp.concatenate(
            [tok_ref[(part * 4 + w) * QP : (part * 4 + w + 1) * QP, :] for part in range(4)], axis=0
        )
        normed = normalize(tokens, gain_one)
        both = dot(normed, wqk)
        query = both[:, :C] * QSCALE
        keys = both[:, C:].astype(BF16)
        values = with_ones(dot(normed, wv))
        items = [
            (keys, values, query[part * QP : (part + 1) * QP],
             lambda chunk=w * 4 + part: dot(joined(wide_ref.at[chunk]).astype(BF16), select))
            for part in range(4)
        ]
        for part, out in enumerate(attend(items)):
            o_ref[(part * 4 + w) * QP : (part * 4 + w + 1) * QP, :] = out
    tok_ref[...] = feed_forward(
        tok_ref[...], o_ref[...].astype(BF16), gain_two, wproj_ref[0], wup_ref[0], wdown_ref[0]
    )
    for part in range(4):
        for w in range(4):
            at = (part * 4 + w) * QP
            for t, tile in enumerate(tiles_of(tok_ref[at : at + QB, :])):
                plain_ref[part, t, pl.ds(w * QB, QB), :] = tile
                if w == 0:
                    plain_ref[part, t, pl.ds(QUAD, 18), :] = tile[:18]
    even = lax.axis_index("lon") % 2 == 0
    for a in range(2):
        for zw in range(4):
            rows = pl.ds(zw * QB + 18, QP)
            left, right = (
                whole_row(plain_ref[a * 2 + b, 0, rows, :], plain_ref[a * 2 + b, 1, rows, :]) for b in range(2)
            )
            fast_ref[a, zw] = jnp.where(even, right, left).astype(BF16)
            slow_ref[a, zw] = jnp.where(even, left, right).astype(BF16)


def bias_kernel(tab_ref, prev_tab_ref, select_ref, bias_ref, rows_ref, work_ref, tv_ref, sems):
    fetch = Fetch(sems)
    fetch.start("own", tab_ref.at[1], tv_ref.at[1])
    fetch.start("prev", prev_tab_ref.at[1], tv_ref.at[0])
    fetch.wait("own", "prev")
    select = select_ref[...].astype(BF16)
    lane = lax.broadcasted_iota(jnp.int32, (QL, 128), 1) + 256
    zi = (lax.broadcasted_iota(jnp.int32, (QL, 1), 0) % QP) // 18
    pen_z = jnp.where(((lane == PEN) & (zi == 1)) | ((lane == PEN + 1) & (zi == 0)), BIG, 0.0)
    lane_row = lane[:1]
    pens = (
        jnp.where((lane_row == PEN + 2) & (lax.axis_index("lat") == 0), BIG, 0.0),
        jnp.where((lane_row == PEN + 3) & (lax.axis_index("lat") == lax.axis_size("lat") - 1), BIG, 0.0),
    )
    for zw in range(4):
        for a in range(2):
            table_rows(tv_ref[a, zw, :, 0, :] * LOG2E, 1 - a, rows_ref.at[a])
            rows = joined(rows_ref.at[a])
            for b in range(2):
                slot = (zw % 2) * 4 + b * 2 + a
                expand_rows(rows, (1 - b) * HLON, slot, work_ref)
                tail = work_ref[slot, 2] + pens[a]
                if zw == 3:
                    tail = tail + pen_z
                wide = jnp.concatenate([work_ref[slot, 0], work_ref[slot, 1], tail], axis=1)
                bias_ref[(b * 2 + a) * 4 + zw] = dot(wide.astype(BF16), select).astype(BF16)


def second_kernel(
    fast_any, slow_any, from_fast_any, from_slow_any, lat_fast_any, lat_slow_any, bias_any,
    gains_ref, wqkv_any, wproj_any, wup_any, wdown_any,
    out_ref,
    plain_ref, own_ref, o_ref,
    near_ref, vert_ref, bias_ref,
    qkv_ref, proj_ref, up_ref, down_ref, sems,
):
    fetch = Fetch(sems)
    even = 1 - lax.axis_index("lon") % 2
    lat_even = 1 - lax.axis_index("lat") % 2
    columns = (1 + even, 2 - even, 3 * even, 3 - 3 * even)
    sides = (fast_any, slow_any, from_fast_any, from_slow_any)
    for i in range(2):
        fetch.start(f"near{i}", sides[i], near_ref.at[columns[i]])
    fetch.start("qkv", wqkv_any.at[1], qkv_ref)
    for i in range(2, 4):
        fetch.start(f"near{i}", sides[i], near_ref.at[columns[i]])
    for i in range(4):
        fetch.start(f"fast{i}", lat_fast_any.at[i], vert_ref.at[lat_even, columns[i]])
        fetch.start(f"slow{i}", lat_slow_any.at[i], vert_ref.at[1 - lat_even, columns[i]])
    fetch.start("bias", bias_any, bias_ref)
    fetch.start("proj", wproj_any.at[1], proj_ref)
    fetch.start("up", wup_any.at[1], up_ref)
    fetch.start("down", wdown_any.at[1], down_ref)
    gain_one = gains_ref[1, 0:1]
    gain_two = gains_ref[1, 1:2]
    fetch.wait("near0", "near1", "qkv")
    wq = qkv_ref[:, :C]
    wk = qkv_ref[:, C : 2 * C]
    wv = value_weights(qkv_ref)
    for b in range(2):
        for a in range(2):
            for zw in range(4):
                at = ((b * 2 + a) * 4 + zw) * QP
                own_ref[at : at + QP, :] = near_ref[1 + b, a, zw].astype(F32)
    query = dot(normalize(own_ref[...], gain_one), wq) * QSCALE
    fetch.wait("near2", "near3", "bias")
    fetch.wait(*[f"{kind}{i}" for kind in ("fast", "slow") for i in range(4)])
    above = [vert_ref.at[0, i] for i in range(4)]
    here = [[near_ref.at[i, a] for i in range(4)] for a in range(2)]
    below = [vert_ref.at[1, i] for i in range(4)]
    for b in range(2):
        for a in range(2):
            pair = (above, here[0]) if a == 0 else (here[1], below)
            sources = [pair[part // 2][b * 2 + part % 2] for part in range(4)]
            items = []
            for zw in range(4):
                chunk = (b * 2 + a) * 4 + zw
                tokens = jnp.concatenate([src[zw].astype(F32) for src in sources], axis=0)
                normed = normalize(tokens, gain_one)
                keys = dot(normed, wk).astype(BF16)
                values = with_ones(dot(normed, wv))
                items.append(
                    (keys, values, query[chunk * QP : (chunk + 1) * QP],
                     lambda chunk=chunk: bias_ref[chunk].astype(F32))
                )
            for zw, out in enumerate(attend(items)):
                chunk = (b * 2 + a) * 4 + zw
                o_ref[chunk * QP : (chunk + 1) * QP, :] = out
    fetch.wait("proj", "up", "down")
    own_ref[...] = feed_forward(
        own_ref[...], o_ref[...].astype(BF16), gain_two, proj_ref[...], up_ref[...], down_ref[...]
    )
    for part in range(4):
        a, b = divmod(part, 2)
        for zw in range(4):
            at = ((b * 2 + a) * 4 + zw) * QP
            for t, tile in enumerate(tiles_of(own_ref[at : at + QB, :])):
                if zw < 3:
                    plain_ref[part, t, pl.ds(zw * QB + 18, QB), :] = tile
                else:
                    plain_ref[part, t, pl.ds(zw * QB + 18, 18), :] = tile[:18]
                    plain_ref[part, t, pl.ds(0, 18), :] = tile[18:]
    for r in range(WLAT):
        for o in range(WLON):
            part = r // HLAT * 2 + o // HLON
            at = (r % HLAT) * 6 + o % HLON
            out_ref[r, o] = whole_row(
                plain_ref[part, 0, pl.ds(at, Z, stride=18), :], plain_ref[part, 1, pl.ds(at, Z, stride=18), :]
            ).astype(BF16)


def whole(shape):
    return pl.BlockSpec(shape, lambda *_: (0,) * len(shape))


ANY = pl.BlockSpec(memory_space=pl.ANY)


def picked(shape, layer):
    return pl.BlockSpec((1,) + shape[1:], lambda *_: (layer,) + (0,) * (len(shape) - 1))


def weight_specs(layer, gains, w_qkv, w_proj, w_up, w_down):
    return [whole(gains.shape)] + [picked(w.shape, layer) for w in (w_qkv, w_proj, w_up, w_down)]


PARAMS = pltpu.CompilerParams(vmem_limit_bytes=56 * 1024 * 1024)


def shifted(value, axis, steps):
    count = lax.axis_size(axis)
    pairs = [(source, (source + steps) % count) for source in range(count)]
    return lax.ppermute(value, axis, pairs)


def paired(axis, first):
    count = lax.axis_size(axis)
    return [(i, (i + 1 if (i + first) % 2 == 0 else i - 1) % count) for i in range(count)]


def call(kernel, name, in_specs, outs, scratch, args):
    single = not isinstance(outs, list)
    specs = [whole(o.shape) for o in (outs if not single else [outs])]
    return pl.pallas_call(
        kernel,
        grid=(1,),
        in_specs=in_specs,
        out_specs=specs[0] if single else specs,
        out_shape=outs,
        scratch_shapes=scratch,
        compiler_params=PARAMS,
        name=name,
    )(*args)


def shards(grid, gains, w_qkv, w_proj, w_up, w_down, tables):
    grid = grid.transpose(1, 2, 0, 3)
    w_down = w_down.transpose(0, 2, 1)
    tables = tables.transpose(0, 1, 3, 2, 4)
    prev_tables = shifted(tables, "lat", 1)
    plain = jnp.asarray(key_select(False))
    masked = jnp.asarray(key_select(True))
    weights = (gains, w_qkv, w_proj, w_up, w_down)
    half = jax.ShapeDtypeStruct((2, 4, QP, C), BF16)
    tok = pltpu.VMEM((16 * QP, C), F32)
    plain_tok = pltpu.VMEM((4, 2, TSPAN, 128), F32)
    table_work = pltpu.VMEM((2, TILES, 48, 128), F32)
    weight_mem = [pltpu.VMEM(w.shape[1:], BF16) for w in weights[1:]]
    fast, slow = call(
        first_kernel, "first_layer",
        [whole(grid.shape)] + weight_specs(0, *weights) + [picked(tables.shape, 0), whole(plain.shape)],
        [half, half],
        [plain_tok, tok, tok, table_work, pltpu.VMEM((16, TILES, QL, 128), F32)],
        (grid, *weights, tables, plain),
    )
    from_fast = lax.ppermute(fast, "lon", paired("lon", 0))
    from_slow = lax.ppermute(slow, "lon", paired("lon", 1))
    from_fast, from_slow, prev_tables = lax.optimization_barrier((from_fast, from_slow, prev_tables))
    bias = call(
        bias_kernel, "second_bias",
        [ANY, ANY, whole(masked.shape)],
        jax.ShapeDtypeStruct((16, QL, SP), BF16),
        [table_work, pltpu.VMEM((8, TILES, QL, 128), F32),
         pltpu.VMEM((2,) + tables.shape[1:], F32), pltpu.SemaphoreType.DMA((2,))],
        (tables, prev_tables, masked),
    )
    odd = lax.axis_index("lat") % 2
    sides = (fast, slow, from_fast, from_slow)
    toward_fast = jnp.concatenate([lax.dynamic_slice_in_dim(v, 1 - odd, 1, 0) for v in sides])
    toward_slow = jnp.concatenate([lax.dynamic_slice_in_dim(v, odd, 1, 0) for v in sides])
    lat_fast = lax.ppermute(toward_fast, "lat", paired("lat", 0))
    lat_slow = lax.ppermute(toward_slow, "lat", paired("lat", 1))
    moved = (*sides, lat_fast, lat_slow, bias)
    out = call(
        second_kernel, "second_layer",
        [ANY] * 7 + [whole(gains.shape)] + [ANY] * 4,
        jax.ShapeDtypeStruct(grid.shape, BF16),
        [plain_tok, tok, tok]
        + [pltpu.VMEM((4,) + half.shape, BF16), pltpu.VMEM((2, 4) + half.shape[1:], BF16), pltpu.VMEM(bias.shape, BF16)]
        + weight_mem + [pltpu.SemaphoreType.DMA((17,))],
        (*moved, *weights),
    )
    return out.transpose(2, 0, 1, 3)


def solution(mesh):
    in_specs = (
        P(None, "lat", "lon", None),
        P(),
        P(),
        P(),
        P(),
        P(),
        P(None, None, "lat", None, None),
    )
    out_specs = P(None, "lat", "lon", None)
    return jax.shard_map(shards, mesh=mesh, in_specs=in_specs, out_specs=out_specs, check_vma=False)
```

```python
import functools
import math

import jax
import jax.numpy as jnp
import numpy as np
from jax import lax
from jax.experimental import pallas as pl
from jax.experimental.pallas import tpu as pltpu
from jax.sharding import PartitionSpec as P

C = 192
HEADS = 6
HEAD = 32
FF = 768
Z = 8
WZ = 2
WLAT = 6
WLON = 12
HLAT = 3
HLON = 6
SPAN = WZ * WLAT * WLON
QB = WZ * HLAT * HLON
QUAD = Z * HLAT * HLON
BAND = 2 * WLON - 1
TROW = WLAT * BAND
TW = 384
TILES = TW // 128
QP = 40
SP = 4 * QP
QL = HEADS * QP
PEN = 300
ONE = 330
TSPAN = 168

EPS = 1e-05
LOG2E = math.log2(math.e)
BIG = -1e30
F32 = jnp.float32
BF16 = jnp.bfloat16
NT = (((1,), (1,)), ((), ()))


def key_select(masked):
    sel = np.zeros((TW, SP), np.float32)
    for part in range(4):
        for zj in range(WZ):
            for r in range(HLAT):
                for o in range(HLON):
                    col = part * QP + zj * 18 + r * 6 + o
                    rj = part // 2 * HLAT + r
                    oj = part % 2 * HLON + o
                    sel[zj * TROW + rj * BAND + oj + WLON - 1, col] = 1
                    if masked:
                        sel[PEN + zj, col] = 1
                        sel[PEN + 2 + part // 2, col] = 1
        sel[ONE : ONE + WLON, part * QP + QB : (part + 1) * QP] = BIG
    return sel


def normalize(values, gain):
    mean = jnp.mean(values, axis=-1, keepdims=True)
    centered = values - mean
    var = jnp.mean(centered * centered, axis=-1, keepdims=True)
    return (centered * lax.rsqrt(var + EPS) * gain).astype(BF16)


def dot(a, b):
    return jnp.dot(a, b, preferred_element_type=F32)


def dot_nt(a, b):
    return lax.dot_general(a, b, NT, preferred_element_type=F32)


def table_rows(table, half, rows_ref):
    blank = jnp.zeros((HEADS, TW - 2 * TROW), F32)
    lane = lax.broadcasted_iota(jnp.int32, blank.shape, 1) + 2 * TROW
    blank = jnp.where(lane == ONE, 1.0, blank)
    for zi in range(WZ):
        for r in range(HLAT):
            at = [((zi * WZ + zj) * WLAT + half * HLAT + r) * TROW for zj in range(WZ)]
            wide = jnp.concatenate([table[:, k : k + TROW] for k in at] + [blank], axis=1)
            for t in range(TILES):
                rows_ref[t, pl.ds(zi * HLAT + r, HEADS, stride=8), :] = (
                    wide[:, t * 128 : (t + 1) * 128]
                )


def joined(tiles):
    return jnp.concatenate([tiles[t] for t in range(TILES)], axis=-1)


def expand_rows(rows, first, chunk, wide_ref):
    for o in range(HLON):
        shift = first + o
        rolled = pltpu.roll(rows, shift, 1) if shift else rows
        for h in range(HEADS):
            for t in range(TILES):
                wide_ref[chunk, t, pl.ds(h * QP + o, 6, stride=6), :] = (
                    rolled[h * 8 : h * 8 + 6, t * 128 : (t + 1) * 128]
                )


def head_lanes():
    lanes = lax.broadcasted_iota(jnp.int32, (1, C), 1)
    return [(lanes >= h * HEAD) & (lanes < (h + 1) * HEAD) for h in range(HEADS)]


def attend(items):
    own = head_lanes()
    stacks = [
        jnp.concatenate([jnp.where(own[h], q, 0.0) for h in range(HEADS)], axis=0).astype(BF16)
        for _, _, q, _ in items
    ]
    scores = [dot_nt(st, it[0]) + it[3]() for st, it in zip(stacks, items)]
    weights = [
        jnp.exp2(s - jnp.max(s, axis=1, keepdims=True)).astype(BF16) for s in scores
    ]
    mixed = [dot(p, it[1]) for p, it in zip(weights, items)]
    outs = []
    for m in mixed:
        scaled = m[:, :C] * (1.0 / m[:, C : C + 1])
        out = scaled[:QP]
        for h in range(1, HEADS):
            out = jnp.where(own[h], scaled[h * QP : (h + 1) * QP], out)
        outs.append(out)
    return outs


class Fetch:
    def __init__(self, sems):
        self.sems = sems
        self.copies = {}

    def start(self, name, source, target):
        copy = pltpu.make_async_copy(source, target, self.sems.at[len(self.copies)])
        self.copies[name] = copy
        copy.start()

    def wait(self, *names):
        for name in names:
            self.copies[name].wait()


def feed_forward(resid, mixed, gain_two, w_proj, w_up, w_down_t):
    first = (resid + dot(mixed, w_proj)).astype(BF16)
    first32 = first.astype(F32)
    inner = normalize(first32, gain_two)
    hidden = dot(inner, w_up)
    hidden = (hidden * 0.5 * (1.0 + lax.erf(hidden * (0.5**0.5)))).astype(BF16)
    return first32 + dot_nt(hidden, w_down_t)


QSCALE = HEAD**-0.5 * LOG2E


def with_ones(values):
    lanes = lax.broadcasted_iota(jnp.int32, values.shape, 1)
    return jnp.where(lanes == C, 1.0, values).astype(BF16)


def value_weights(qkv_ref):
    return jnp.concatenate([qkv_ref[:, 2 * C :], jnp.zeros((C, 256 - C), BF16)], axis=1)


def tiles_of(value):
    return value[:, :128], jnp.concatenate([value[:, 128:], value[:, 128:]], axis=1)


def whole_row(first, second):
    return jnp.concatenate([first, second[:, : C - 128]], axis=1)


def first_kernel(
    x_ref, gains_ref, wqkv_ref, wproj_ref, wup_ref, wdown_ref, tab_ref,
    select_ref,
    fast_ref, slow_ref,
    plain_ref, tok_ref, o_ref, rows_ref, wide_ref,
):
    plain_ref[...] = jnp.zeros_like(plain_ref)
    for r in range(WLAT):
        for o in range(WLON):
            part = r // HLAT * 2 + o // HLON
            at = (r % HLAT) * 6 + o % HLON
            for t, tile in enumerate(tiles_of(x_ref[r, o].astype(F32))):
                plain_ref[part, t, pl.ds(at, Z, stride=18), :] = tile
    for part in range(4):
        for w in range(4):
            rows = pl.ds(w * QB, QP)
            at = (part * 4 + w) * QP
            tok_ref[at : at + QP, :] = whole_row(plain_ref[part, 0, rows, :], plain_ref[part, 1, rows, :])
    select = select_ref[...].astype(BF16)
    for w in range(4):
        table = tab_ref[0, w, :, 0, :] * LOG2E
        for a in range(2):
            table_rows(table, a, rows_ref.at[a])
            rows = joined(rows_ref.at[a])
            for b in range(2):
                expand_rows(rows, b * HLON, w * 4 + a * 2 + b, wide_ref)
    gain_one = gains_ref[0, 0:1]
    gain_two = gains_ref[0, 1:2]
    wqk = wqkv_ref[0, :, : 2 * C]
    wv = value_weights(wqkv_ref.at[0])
    for w in range(4):
        tokens = jnp.concatenate(
            [tok_ref[(part * 4 + w) * QP : (part * 4 + w + 1) * QP, :] for part in range(4)], axis=0
        )
        normed = normalize(tokens, gain_one)
        both = dot(normed, wqk)
        query = both[:, :C] * QSCALE
        keys = both[:, C:].astype(BF16)
        values = with_ones(dot(normed, wv))
        items = [
            (keys, values, query[part * QP : (part + 1) * QP],
             lambda chunk=w * 4 + part: dot(joined(wide_ref.at[chunk]).astype(BF16), select))
            for part in range(4)
        ]
        for part, out in enumerate(attend(items)):
            o_ref[(part * 4 + w) * QP : (part * 4 + w + 1) * QP, :] = out
    tok_ref[...] = feed_forward(
        tok_ref[...], o_ref[...].astype(BF16), gain_two, wproj_ref[0], wup_ref[0], wdown_ref[0]
    )
    for part in range(4):
        for w in range(4):
            at = (part * 4 + w) * QP
            for t, tile in enumerate(tiles_of(tok_ref[at : at + QB, :])):
                plain_ref[part, t, pl.ds(w * QB, QB), :] = tile
                if w == 0:
                    plain_ref[part, t, pl.ds(QUAD, 18), :] = tile[:18]
    even = lax.axis_index("lon") % 2 == 0
    low = lax.broadcasted_iota(jnp.int32, (QP, 128), 1) < 128 - (C - 128)
    for a in range(2):
        for pair in range(2):
            rows = [pl.ds((pair * 2 + k) * QB + 18, QP) for k in range(2)]
            sides = []
            for b in range(2):
                part = a * 2 + b
                lasts = [plain_ref[part, 1, r, :] for r in rows]
                sides.append([plain_ref[part, 0, r, :] for r in rows] + [jnp.where(low, lasts[0], lasts[1])])
            for k, (left, right) in enumerate(zip(*sides)):
                fast_ref[a, pair * 3 + k] = jnp.where(even, right, left).astype(BF16)
                slow_ref[a, pair * 3 + k] = jnp.where(even, left, right).astype(BF16)


def block_of(tiles_ref, zw):
    pair, second = divmod(zw, 2)
    last = tiles_ref[pair * 3 + 2].astype(F32)
    if second:
        last = pltpu.roll(last, 64, 1)
    return whole_row(tiles_ref[pair * 3 + second].astype(F32), last)


def bias_kernel(tab_ref, prev_tab_ref, select_ref, bias_ref, rows_ref, work_ref, tv_ref, sems):
    fetch = Fetch(sems)
    fetch.start("own", tab_ref.at[1], tv_ref.at[1])
    fetch.start("prev", prev_tab_ref.at[1], tv_ref.at[0])
    fetch.wait("own", "prev")
    select = select_ref[...].astype(BF16)
    lane = lax.broadcasted_iota(jnp.int32, (QL, 128), 1) + 256
    zi = (lax.broadcasted_iota(jnp.int32, (QL, 1), 0) % QP) // 18
    pen_z = jnp.where(((lane == PEN) & (zi == 1)) | ((lane == PEN + 1) & (zi == 0)), BIG, 0.0)
    lane_row = lane[:1]
    pens = (
        jnp.where((lane_row == PEN + 2) & (lax.axis_index("lat") == 0), BIG, 0.0),
        jnp.where((lane_row == PEN + 3) & (lax.axis_index("lat") == lax.axis_size("lat") - 1), BIG, 0.0),
    )
    for zw in range(4):
        for a in range(2):
            table_rows(tv_ref[a, zw, :, 0, :] * LOG2E, 1 - a, rows_ref.at[a])
            rows = joined(rows_ref.at[a])
            for b in range(2):
                slot = (zw % 2) * 4 + b * 2 + a
                expand_rows(rows, (1 - b) * HLON, slot, work_ref)
                tail = work_ref[slot, 2] + pens[a]
                if zw == 3:
                    tail = tail + pen_z
                wide = jnp.concatenate([work_ref[slot, 0], work_ref[slot, 1], tail], axis=1)
                bias_ref[(b * 2 + a) * 4 + zw] = dot(wide.astype(BF16), select).astype(BF16)


def second_kernel(
    fast_any, slow_any, from_fast_any, from_slow_any, lat_fast_any, lat_slow_any, bias_any,
    gains_ref, wqkv_any, wproj_any, wup_any, wdown_any,
    out_ref,
    plain_ref, own_ref, o_ref,
    near_ref, vert_ref, bias_ref,
    qkv_ref, proj_ref, up_ref, down_ref, sems,
):
    fetch = Fetch(sems)
    even = 1 - lax.axis_index("lon") % 2
    lat_even = 1 - lax.axis_index("lat") % 2
    columns = (1 + even, 2 - even, 3 * even, 3 - 3 * even)
    sides = (fast_any, slow_any, from_fast_any, from_slow_any)
    for i in range(2):
        fetch.start(f"near{i}", sides[i], near_ref.at[columns[i]])
    fetch.start("qkv", wqkv_any.at[1], qkv_ref)
    for i in range(2, 4):
        fetch.start(f"near{i}", sides[i], near_ref.at[columns[i]])
    for i in range(4):
        fetch.start(f"fast{i}", lat_fast_any.at[i], vert_ref.at[lat_even, columns[i]])
        fetch.start(f"slow{i}", lat_slow_any.at[i], vert_ref.at[1 - lat_even, columns[i]])
    fetch.start("bias", bias_any, bias_ref)
    fetch.start("proj", wproj_any.at[1], proj_ref)
    fetch.start("up", wup_any.at[1], up_ref)
    fetch.start("down", wdown_any.at[1], down_ref)
    gain_one = gains_ref[1, 0:1]
    gain_two = gains_ref[1, 1:2]
    fetch.wait("near0", "near1", "qkv")
    wq = qkv_ref[:, :C]
    wk = qkv_ref[:, C : 2 * C]
    wv = value_weights(qkv_ref)
    for b in range(2):
        for a in range(2):
            for zw in range(4):
                at = ((b * 2 + a) * 4 + zw) * QP
                own_ref[at : at + QP, :] = block_of(near_ref.at[1 + b, a], zw)
    query = dot(normalize(own_ref[...], gain_one), wq) * QSCALE
    fetch.wait("near2", "near3", "bias")
    fetch.wait(*[f"{kind}{i}" for kind in ("fast", "slow") for i in range(4)])
    above = [vert_ref.at[0, i] for i in range(4)]
    here = [[near_ref.at[i, a] for i in range(4)] for a in range(2)]
    below = [vert_ref.at[1, i] for i in range(4)]
    for b in range(2):
        for a in range(2):
            pair = (above, here[0]) if a == 0 else (here[1], below)
            sources = [pair[part // 2][b * 2 + part % 2] for part in range(4)]
            items = []
            for zw in range(4):
                chunk = (b * 2 + a) * 4 + zw
                tokens = jnp.concatenate([block_of(src, zw) for src in sources], axis=0)
                normed = normalize(tokens, gain_one)
                keys = dot(normed, wk).astype(BF16)
                values = with_ones(dot(normed, wv))
                items.append(
                    (keys, values, query[chunk * QP : (chunk + 1) * QP],
                     lambda chunk=chunk: bias_ref[chunk].astype(F32))
                )
            for zw, out in enumerate(attend(items)):
                chunk = (b * 2 + a) * 4 + zw
                o_ref[chunk * QP : (chunk + 1) * QP, :] = out
    fetch.wait("proj", "up", "down")
    own_ref[...] = feed_forward(
        own_ref[...], o_ref[...].astype(BF16), gain_two, proj_ref[...], up_ref[...], down_ref[...]
    )
    for part in range(4):
        a, b = divmod(part, 2)
        for zw in range(4):
            at = ((b * 2 + a) * 4 + zw) * QP
            for t, tile in enumerate(tiles_of(own_ref[at : at + QB, :])):
                if zw < 3:
                    plain_ref[part, t, pl.ds(zw * QB + 18, QB), :] = tile
                else:
                    plain_ref[part, t, pl.ds(zw * QB + 18, 18), :] = tile[:18]
                    plain_ref[part, t, pl.ds(0, 18), :] = tile[18:]
    for r in range(WLAT):
        for o in range(WLON):
            part = r // HLAT * 2 + o // HLON
            at = (r % HLAT) * 6 + o % HLON
            out_ref[r, o] = whole_row(
                plain_ref[part, 0, pl.ds(at, Z, stride=18), :], plain_ref[part, 1, pl.ds(at, Z, stride=18), :]
            ).astype(BF16)


def whole(shape):
    return pl.BlockSpec(shape, lambda *_: (0,) * len(shape))


ANY = pl.BlockSpec(memory_space=pl.ANY)


def picked(shape, layer):
    return pl.BlockSpec((1,) + shape[1:], lambda *_: (layer,) + (0,) * (len(shape) - 1))


def weight_specs(layer, gains, w_qkv, w_proj, w_up, w_down):
    return [whole(gains.shape)] + [picked(w.shape, layer) for w in (w_qkv, w_proj, w_up, w_down)]


PARAMS = pltpu.CompilerParams(vmem_limit_bytes=56 * 1024 * 1024)


def shifted(value, axis, steps):
    count = lax.axis_size(axis)
    pairs = [(source, (source + steps) % count) for source in range(count)]
    return lax.ppermute(value, axis, pairs)


def paired(axis, first):
    count = lax.axis_size(axis)
    return [(i, (i + 1 if (i + first) % 2 == 0 else i - 1) % count) for i in range(count)]


def call(kernel, name, in_specs, outs, scratch, args):
    single = not isinstance(outs, list)
    specs = [whole(o.shape) for o in (outs if not single else [outs])]
    return pl.pallas_call(
        kernel,
        grid=(1,),
        in_specs=in_specs,
        out_specs=specs[0] if single else specs,
        out_shape=outs,
        scratch_shapes=scratch,
        compiler_params=PARAMS,
        name=name,
    )(*args)


def shards(grid, gains, w_qkv, w_proj, w_up, w_down, tables):
    grid = grid.transpose(1, 2, 0, 3)
    w_down = w_down.transpose(0, 2, 1)
    tables = tables.transpose(0, 1, 3, 2, 4)
    prev_tables = shifted(tables, "lat", 1)
    plain = jnp.asarray(key_select(False))
    masked = jnp.asarray(key_select(True))
    weights = (gains, w_qkv, w_proj, w_up, w_down)
    half = jax.ShapeDtypeStruct((2, 6, QP, 128), BF16)
    tok = pltpu.VMEM((16 * QP, C), F32)
    plain_tok = pltpu.VMEM((4, 2, TSPAN, 128), F32)
    table_work = pltpu.VMEM((2, TILES, 48, 128), F32)
    weight_mem = [pltpu.VMEM(w.shape[1:], BF16) for w in weights[1:]]
    fast, slow = call(
        first_kernel, "first_layer",
        [whole(grid.shape)] + weight_specs(0, *weights) + [picked(tables.shape, 0), whole(plain.shape)],
        [half, half],
        [plain_tok, tok, tok, table_work, pltpu.VMEM((16, TILES, QL, 128), F32)],
        (grid, *weights, tables, plain),
    )
    from_fast = lax.ppermute(fast, "lon", paired("lon", 0))
    from_slow = lax.ppermute(slow, "lon", paired("lon", 1))
    from_fast, from_slow, prev_tables = lax.optimization_barrier((from_fast, from_slow, prev_tables))
    bias = call(
        bias_kernel, "second_bias",
        [ANY, ANY, whole(masked.shape)],
        jax.ShapeDtypeStruct((16, QL, SP), BF16),
        [table_work, pltpu.VMEM((8, TILES, QL, 128), F32),
         pltpu.VMEM((2,) + tables.shape[1:], F32), pltpu.SemaphoreType.DMA((2,))],
        (tables, prev_tables, masked),
    )
    odd = lax.axis_index("lat") % 2
    sides = (fast, slow, from_fast, from_slow)
    toward_fast = jnp.concatenate([lax.dynamic_slice_in_dim(v, 1 - odd, 1, 0) for v in sides])
    toward_slow = jnp.concatenate([lax.dynamic_slice_in_dim(v, odd, 1, 0) for v in sides])
    lat_fast = lax.ppermute(toward_fast, "lat", paired("lat", 0))
    lat_slow = lax.ppermute(toward_slow, "lat", paired("lat", 1))
    moved = (*sides, lat_fast, lat_slow, bias)
    out = call(
        second_kernel, "second_layer",
        [ANY] * 7 + [whole(gains.shape)] + [ANY] * 4,
        jax.ShapeDtypeStruct(grid.shape, BF16),
        [plain_tok, tok, tok]
        + [pltpu.VMEM((4,) + half.shape, BF16), pltpu.VMEM((2, 4) + half.shape[1:], BF16), pltpu.VMEM(bias.shape, BF16)]
        + weight_mem + [pltpu.SemaphoreType.DMA((17,))],
        (*moved, *weights),
    )
    return out.transpose(2, 0, 1, 3)


def solution(mesh):
    in_specs = (
        P(None, "lat", "lon", None),
        P(),
        P(),
        P(),
        P(),
        P(),
        P(None, None, "lat", None, None),
    )
    out_specs = P(None, "lat", "lon", None)
    return jax.shard_map(shards, mesh=mesh, in_specs=in_specs, out_specs=out_specs, check_vma=False)
```

```python
import functools
import math

import jax
import jax.numpy as jnp
import numpy as np
from jax import lax
from jax.experimental import pallas as pl
from jax.experimental.pallas import tpu as pltpu
from jax.sharding import PartitionSpec as P

C = 192
HEADS = 6
HEAD = 32
FF = 768
Z = 8
WZ = 2
WLAT = 6
WLON = 12
HLAT = 3
HLON = 6
SPAN = WZ * WLAT * WLON
QB = WZ * HLAT * HLON
QUAD = Z * HLAT * HLON
BAND = 2 * WLON - 1
TROW = WLAT * BAND
TW = 384
TILES = TW // 128
QP = 40
SP = 4 * QP
QL = HEADS * QP
PEN = 300
ONE = 330
TSPAN = 168

EPS = 1e-05
LOG2E = math.log2(math.e)
BIG = -1e30
F32 = jnp.float32
BF16 = jnp.bfloat16
NT = (((1,), (1,)), ((), ()))


def key_select(masked):
    sel = np.zeros((TW, SP), np.float32)
    for part in range(4):
        for zj in range(WZ):
            for r in range(HLAT):
                for o in range(HLON):
                    col = part * QP + zj * 18 + r * 6 + o
                    rj = part // 2 * HLAT + r
                    oj = part % 2 * HLON + o
                    sel[zj * TROW + rj * BAND + oj + WLON - 1, col] = 1
                    if masked:
                        sel[PEN + zj, col] = 1
                        sel[PEN + 2 + part // 2, col] = 1
        sel[ONE : ONE + WLON, part * QP + QB : (part + 1) * QP] = BIG
    return sel


def normalize(values, gain):
    mean = jnp.mean(values, axis=-1, keepdims=True)
    centered = values - mean
    var = jnp.mean(centered * centered, axis=-1, keepdims=True)
    return (centered * lax.rsqrt(var + EPS) * gain).astype(BF16)


def dot(a, b):
    return jnp.dot(a, b, preferred_element_type=F32)


def dot_nt(a, b):
    return lax.dot_general(a, b, NT, preferred_element_type=F32)


def table_rows(table, half, rows_ref):
    blank = jnp.zeros((HEADS, TW - 2 * TROW), F32)
    lane = lax.broadcasted_iota(jnp.int32, blank.shape, 1) + 2 * TROW
    blank = jnp.where(lane == ONE, 1.0, blank)
    for zi in range(WZ):
        for r in range(HLAT):
            at = [((zi * WZ + zj) * WLAT + half * HLAT + r) * TROW for zj in range(WZ)]
            wide = jnp.concatenate([table[:, k : k + TROW] for k in at] + [blank], axis=1)
            for t in range(TILES):
                rows_ref[t, pl.ds(zi * HLAT + r, HEADS, stride=8), :] = (
                    wide[:, t * 128 : (t + 1) * 128]
                )


def joined(tiles):
    return jnp.concatenate([tiles[t] for t in range(TILES)], axis=-1)


def expand_rows(rows, first, chunk, wide_ref):
    for o in range(HLON):
        shift = first + o
        rolled = pltpu.roll(rows, shift, 1) if shift else rows
        for h in range(HEADS):
            for t in range(TILES):
                wide_ref[chunk, t, pl.ds(h * QP + o, 6, stride=6), :] = (
                    rolled[h * 8 : h * 8 + 6, t * 128 : (t + 1) * 128]
                )


def head_lanes():
    lanes = lax.broadcasted_iota(jnp.int32, (1, C), 1)
    return [(lanes >= h * HEAD) & (lanes < (h + 1) * HEAD) for h in range(HEADS)]


def attend(items):
    own = head_lanes()
    stacks = [
        jnp.concatenate([jnp.where(own[h], q, 0.0) for h in range(HEADS)], axis=0).astype(BF16)
        for _, _, q, _ in items
    ]
    scores = [dot_nt(st, it[0]) + it[3]() for st, it in zip(stacks, items)]
    weights = [
        jnp.exp2(s - jnp.max(s, axis=1, keepdims=True)).astype(BF16) for s in scores
    ]
    mixed = [dot(p, it[1]) for p, it in zip(weights, items)]
    outs = []
    for m in mixed:
        scaled = m[:, :C] * (1.0 / m[:, C : C + 1])
        out = scaled[:QP]
        for h in range(1, HEADS):
            out = jnp.where(own[h], scaled[h * QP : (h + 1) * QP], out)
        outs.append(out)
    return outs


class Fetch:
    def __init__(self, sems):
        self.sems = sems
        self.copies = {}

    def start(self, name, source, target):
        copy = pltpu.make_async_copy(source, target, self.sems.at[len(self.copies)])
        self.copies[name] = copy
        copy.start()

    def wait(self, *names):
        for name in names:
            self.copies[name].wait()


def feed_forward(resid, mixed, gain_two, w_proj, w_up, w_down_t):
    first = (resid + dot(mixed, w_proj)).astype(BF16)
    first32 = first.astype(F32)
    inner = normalize(first32, gain_two)
    hidden = dot(inner, w_up)
    hidden = (hidden * 0.5 * (1.0 + lax.erf(hidden * (0.5**0.5)))).astype(BF16)
    return first32 + dot_nt(hidden, w_down_t)


QSCALE = HEAD**-0.5 * LOG2E


def with_ones(values):
    lanes = lax.broadcasted_iota(jnp.int32, values.shape, 1)
    return jnp.where(lanes == C, 1.0, values).astype(BF16)


def value_weights(qkv_ref):
    return jnp.concatenate([qkv_ref[:, 2 * C :], jnp.zeros((C, 256 - C), BF16)], axis=1)


def tiles_of(value):
    return value[:, :128], jnp.concatenate([value[:, 128:], value[:, 128:]], axis=1)


def whole_row(first, second):
    return jnp.concatenate([first, second[:, : C - 128]], axis=1)


def first_kernel(
    x_ref, gains_ref, wqkv_ref, wproj_ref, wup_ref, wdown_ref, tab_ref,
    select_ref,
    fast_ref, slow_ref,
    plain_ref, tok_ref, o_ref, rows_ref, wide_ref,
):
    plain_ref[...] = jnp.zeros_like(plain_ref)
    for r in range(WLAT):
        for o in range(WLON):
            part = r // HLAT * 2 + o // HLON
            at = (r % HLAT) * 6 + o % HLON
            for t, tile in enumerate(tiles_of(x_ref[r, o].astype(F32))):
                plain_ref[part, t, pl.ds(at, Z, stride=18), :] = tile
    for part in range(4):
        for w in range(4):
            rows = pl.ds(w * QB, QP)
            at = (part * 4 + w) * QP
            tok_ref[at : at + QP, :] = whole_row(plain_ref[part, 0, rows, :], plain_ref[part, 1, rows, :])
    select = select_ref[...].astype(BF16)
    for w in range(4):
        table = tab_ref[0, w, :, 0, :] * LOG2E
        for a in range(2):
            table_rows(table, a, rows_ref.at[a])
            rows = joined(rows_ref.at[a])
            for b in range(2):
                expand_rows(rows, b * HLON, w * 4 + a * 2 + b, wide_ref)
    gain_one = gains_ref[0, 0:1]
    gain_two = gains_ref[0, 1:2]
    wqk = wqkv_ref[0, :, : 2 * C]
    wv = value_weights(wqkv_ref.at[0])
    for w in range(4):
        tokens = jnp.concatenate(
            [tok_ref[(part * 4 + w) * QP : (part * 4 + w + 1) * QP, :] for part in range(4)], axis=0
        )
        normed = normalize(tokens, gain_one)
        both = dot(normed, wqk)
        query = both[:, :C] * QSCALE
        keys = both[:, C:].astype(BF16)
        values = with_ones(dot(normed, wv))
        items = [
            (keys, values, query[part * QP : (part + 1) * QP],
             lambda chunk=w * 4 + part: dot(joined(wide_ref.at[chunk]).astype(BF16), select))
            for part in range(4)
        ]
        for part, out in enumerate(attend(items)):
            o_ref[(part * 4 + w) * QP : (part * 4 + w + 1) * QP, :] = out
    tok_ref[...] = feed_forward(
        tok_ref[...], o_ref[...].astype(BF16), gain_two, wproj_ref[0], wup_ref[0], wdown_ref[0]
    )
    for part in range(4):
        for w in range(4):
            at = (part * 4 + w) * QP
            for t, tile in enumerate(tiles_of(tok_ref[at : at + QB, :])):
                plain_ref[part, t, pl.ds(w * QB, QB), :] = tile
                if w == 0:
                    plain_ref[part, t, pl.ds(QUAD, 18), :] = tile[:18]
    even = lax.axis_index("lon") % 2 == 0
    low = lax.broadcasted_iota(jnp.int32, (QP, 128), 1) < 128 - (C - 128)
    for a in range(2):
        for pair in range(2):
            rows = [pl.ds((pair * 2 + k) * QB + 18, QP) for k in range(2)]
            sides = []
            for b in range(2):
                part = a * 2 + b
                lasts = [plain_ref[part, 1, r, :] for r in rows]
                sides.append([plain_ref[part, 0, r, :] for r in rows] + [jnp.where(low, lasts[0], lasts[1])])
            for k, (left, right) in enumerate(zip(*sides)):
                fast_ref[a, pair * 3 + k] = jnp.where(even, right, left).astype(BF16)
                slow_ref[a, pair * 3 + k] = jnp.where(even, left, right).astype(BF16)


def block_of(tiles_ref, zw):
    pair, second = divmod(zw, 2)
    last = tiles_ref[pair * 3 + 2].astype(F32)
    if second:
        last = pltpu.roll(last, 64, 1)
    return whole_row(tiles_ref[pair * 3 + second].astype(F32), last)


def bias_kernel(tab_ref, prev_tab_ref, select_ref, bias_ref, rows_ref, work_ref, tv_ref, sems):
    fetch = Fetch(sems)
    fetch.start("own", tab_ref.at[1], tv_ref.at[1])
    fetch.start("prev", prev_tab_ref.at[1], tv_ref.at[0])
    fetch.wait("own", "prev")
    select = select_ref[...].astype(BF16)
    lane = lax.broadcasted_iota(jnp.int32, (QL, 128), 1) + 256
    zi = (lax.broadcasted_iota(jnp.int32, (QL, 1), 0) % QP) // 18
    pen_z = jnp.where(((lane == PEN) & (zi == 1)) | ((lane == PEN + 1) & (zi == 0)), BIG, 0.0)
    lane_row = lane[:1]
    pens = (
        jnp.where((lane_row == PEN + 2) & (lax.axis_index("lat") == 0), BIG, 0.0),
        jnp.where((lane_row == PEN + 3) & (lax.axis_index("lat") == lax.axis_size("lat") - 1), BIG, 0.0),
    )
    for zw in range(4):
        for a in range(2):
            table_rows(tv_ref[a, zw, :, 0, :] * LOG2E, 1 - a, rows_ref.at[a])
            rows = joined(rows_ref.at[a])
            for b in range(2):
                slot = (zw % 2) * 4 + b * 2 + a
                expand_rows(rows, (1 - b) * HLON, slot, work_ref)
                tail = work_ref[slot, 2] + pens[a]
                if zw == 3:
                    tail = tail + pen_z
                wide = jnp.concatenate([work_ref[slot, 0], work_ref[slot, 1], tail], axis=1)
                bias_ref[(b * 2 + a) * 4 + zw] = dot(wide.astype(BF16), select).astype(BF16)


def holed(value, axis):
    blank = jnp.zeros((value.shape[0], 64) if axis else (64, value.shape[1]), value.dtype)
    head, last = (value[:, :128], value[:, 128:]) if axis else (value[:128], value[128:])
    return (
        jnp.concatenate([head, last, blank], axis=axis),
        jnp.concatenate([head, blank, last], axis=axis),
    )


def holed_normalize(sources, zw, gain):
    pair, second = divmod(zw, 2)
    values = jnp.concatenate(
        [
            jnp.concatenate([src[pair * 3 + second], src[pair * 3 + 2]], axis=1).astype(F32)
            for src in sources
        ],
        axis=0,
    )
    lanes = lax.broadcasted_iota(jnp.int32, (1, 256), 1)
    there = (lanes < 128) | (lanes >= 192) if second else lanes < C
    mean = jnp.sum(jnp.where(there, values, 0.0), axis=-1, keepdims=True) * (1.0 / C)
    centered = jnp.where(there, values - mean, 0.0)
    var = jnp.sum(centered * centered, axis=-1, keepdims=True) * (1.0 / C)
    return (centered * lax.rsqrt(var + EPS) * gain).astype(BF16)


def second_kernel(
    fast_any, slow_any, from_fast_any, from_slow_any, lat_fast_any, lat_slow_any, bias_any,
    gains_ref, wqkv_any, wproj_any, wup_any, wdown_any,
    out_ref,
    plain_ref, own_ref, o_ref,
    near_ref, vert_ref, bias_ref,
    qkv_ref, proj_ref, up_ref, down_ref, sems,
):
    fetch = Fetch(sems)
    even = 1 - lax.axis_index("lon") % 2
    lat_even = 1 - lax.axis_index("lat") % 2
    columns = (1 + even, 2 - even, 3 * even, 3 - 3 * even)
    sides = (fast_any, slow_any, from_fast_any, from_slow_any)
    for i in range(2):
        fetch.start(f"near{i}", sides[i], near_ref.at[columns[i]])
    fetch.start("qkv", wqkv_any.at[1], qkv_ref)
    for i in range(2, 4):
        fetch.start(f"near{i}", sides[i], near_ref.at[columns[i]])
    for i in range(4):
        fetch.start(f"fast{i}", lat_fast_any.at[i], vert_ref.at[lat_even, columns[i]])
        fetch.start(f"slow{i}", lat_slow_any.at[i], vert_ref.at[1 - lat_even, columns[i]])
    fetch.start("bias", bias_any, bias_ref)
    fetch.start("proj", wproj_any.at[1], proj_ref)
    fetch.start("up", wup_any.at[1], up_ref)
    fetch.start("down", wdown_any.at[1], down_ref)
    gain_one = gains_ref[1, 0:1]
    gain_two = gains_ref[1, 1:2]
    fetch.wait("near0", "near1", "qkv")
    wq = qkv_ref[:, :C]
    wk = holed(qkv_ref[:, C : 2 * C], 0)
    wv = holed(value_weights(qkv_ref), 0)
    gains = holed(gain_one, 1)
    for b in range(2):
        for a in range(2):
            for zw in range(4):
                at = ((b * 2 + a) * 4 + zw) * QP
                own_ref[at : at + QP, :] = block_of(near_ref.at[1 + b, a], zw)
    query = dot(normalize(own_ref[...], gain_one), wq) * QSCALE
    fetch.wait("near2", "near3", "bias")
    fetch.wait(*[f"{kind}{i}" for kind in ("fast", "slow") for i in range(4)])
    above = [vert_ref.at[0, i] for i in range(4)]
    here = [[near_ref.at[i, a] for i in range(4)] for a in range(2)]
    below = [vert_ref.at[1, i] for i in range(4)]
    for b in range(2):
        for a in range(2):
            pair = (above, here[0]) if a == 0 else (here[1], below)
            sources = [pair[part // 2][b * 2 + part % 2] for part in range(4)]
            items = []
            for zw in range(4):
                chunk = (b * 2 + a) * 4 + zw
                normed = holed_normalize(sources, zw, gains[zw % 2])
                keys = dot(normed, wk[zw % 2]).astype(BF16)
                values = with_ones(dot(normed, wv[zw % 2]))
                items.append(
                    (keys, values, query[chunk * QP : (chunk + 1) * QP],
                     lambda chunk=chunk: bias_ref[chunk].astype(F32))
                )
            for zw, out in enumerate(attend(items)):
                chunk = (b * 2 + a) * 4 + zw
                o_ref[chunk * QP : (chunk + 1) * QP, :] = out
    fetch.wait("proj", "up", "down")
    own_ref[...] = feed_forward(
        own_ref[...], o_ref[...].astype(BF16), gain_two, proj_ref[...], up_ref[...], down_ref[...]
    )
    for part in range(4):
        a, b = divmod(part, 2)
        for zw in range(4):
            at = ((b * 2 + a) * 4 + zw) * QP
            for t, tile in enumerate(tiles_of(own_ref[at : at + QB, :])):
                if zw < 3:
                    plain_ref[part, t, pl.ds(zw * QB + 18, QB), :] = tile
                else:
                    plain_ref[part, t, pl.ds(zw * QB + 18, 18), :] = tile[:18]
                    plain_ref[part, t, pl.ds(0, 18), :] = tile[18:]
    for r in range(WLAT):
        for o in range(WLON):
            part = r // HLAT * 2 + o // HLON
            at = (r % HLAT) * 6 + o % HLON
            out_ref[r, o] = whole_row(
                plain_ref[part, 0, pl.ds(at, Z, stride=18), :], plain_ref[part, 1, pl.ds(at, Z, stride=18), :]
            ).astype(BF16)


def whole(shape):
    return pl.BlockSpec(shape, lambda *_: (0,) * len(shape))


ANY = pl.BlockSpec(memory_space=pl.ANY)


def picked(shape, layer):
    return pl.BlockSpec((1,) + shape[1:], lambda *_: (layer,) + (0,) * (len(shape) - 1))


def weight_specs(layer, gains, w_qkv, w_proj, w_up, w_down):
    return [whole(gains.shape)] + [picked(w.shape, layer) for w in (w_qkv, w_proj, w_up, w_down)]


PARAMS = pltpu.CompilerParams(vmem_limit_bytes=56 * 1024 * 1024)


def shifted(value, axis, steps):
    count = lax.axis_size(axis)
    pairs = [(source, (source + steps) % count) for source in range(count)]
    return lax.ppermute(value, axis, pairs)


def paired(axis, first):
    count = lax.axis_size(axis)
    return [(i, (i + 1 if (i + first) % 2 == 0 else i - 1) % count) for i in range(count)]


def call(kernel, name, in_specs, outs, scratch, args):
    single = not isinstance(outs, list)
    specs = [whole(o.shape) for o in (outs if not single else [outs])]
    return pl.pallas_call(
        kernel,
        grid=(1,),
        in_specs=in_specs,
        out_specs=specs[0] if single else specs,
        out_shape=outs,
        scratch_shapes=scratch,
        compiler_params=PARAMS,
        name=name,
    )(*args)


def shards(grid, gains, w_qkv, w_proj, w_up, w_down, tables):
    grid = grid.transpose(1, 2, 0, 3)
    w_down = w_down.transpose(0, 2, 1)
    tables = tables.transpose(0, 1, 3, 2, 4)
    prev_tables = shifted(tables, "lat", 1)
    plain = jnp.asarray(key_select(False))
    masked = jnp.asarray(key_select(True))
    weights = (gains, w_qkv, w_proj, w_up, w_down)
    half = jax.ShapeDtypeStruct((2, 6, QP, 128), BF16)
    tok = pltpu.VMEM((16 * QP, C), F32)
    plain_tok = pltpu.VMEM((4, 2, TSPAN, 128), F32)
    table_work = pltpu.VMEM((2, TILES, 48, 128), F32)
    weight_mem = [pltpu.VMEM(w.shape[1:], BF16) for w in weights[1:]]
    fast, slow = call(
        first_kernel, "first_layer",
        [whole(grid.shape)] + weight_specs(0, *weights) + [picked(tables.shape, 0), whole(plain.shape)],
        [half, half],
        [plain_tok, tok, tok, table_work, pltpu.VMEM((16, TILES, QL, 128), F32)],
        (grid, *weights, tables, plain),
    )
    from_fast = lax.ppermute(fast, "lon", paired("lon", 0))
    from_slow = lax.ppermute(slow, "lon", paired("lon", 1))
    from_fast, from_slow, prev_tables = lax.optimization_barrier((from_fast, from_slow, prev_tables))
    bias = call(
        bias_kernel, "second_bias",
        [ANY, ANY, whole(masked.shape)],
        jax.ShapeDtypeStruct((16, QL, SP), BF16),
        [table_work, pltpu.VMEM((8, TILES, QL, 128), F32),
         pltpu.VMEM((2,) + tables.shape[1:], F32), pltpu.SemaphoreType.DMA((2,))],
        (tables, prev_tables, masked),
    )
    odd = lax.axis_index("lat") % 2
    sides = (fast, slow, from_fast, from_slow)
    toward_fast = jnp.concatenate([lax.dynamic_slice_in_dim(v, 1 - odd, 1, 0) for v in sides])
    toward_slow = jnp.concatenate([lax.dynamic_slice_in_dim(v, odd, 1, 0) for v in sides])
    lat_fast = lax.ppermute(toward_fast, "lat", paired("lat", 0))
    lat_slow = lax.ppermute(toward_slow, "lat", paired("lat", 1))
    moved = (*sides, lat_fast, lat_slow, bias)
    out = call(
        second_kernel, "second_layer",
        [ANY] * 7 + [whole(gains.shape)] + [ANY] * 4,
        jax.ShapeDtypeStruct(grid.shape, BF16),
        [plain_tok, tok, tok]
        + [pltpu.VMEM((4,) + half.shape, BF16), pltpu.VMEM((2, 4) + half.shape[1:], BF16), pltpu.VMEM(bias.shape, BF16)]
        + weight_mem + [pltpu.SemaphoreType.DMA((17,))],
        (*moved, *weights),
    )
    return out.transpose(2, 0, 1, 3)


def solution(mesh):
    in_specs = (
        P(None, "lat", "lon", None),
        P(),
        P(),
        P(),
        P(),
        P(),
        P(None, None, "lat", None, None),
    )
    out_specs = P(None, "lat", "lon", None)
    return jax.shard_map(shards, mesh=mesh, in_specs=in_specs, out_specs=out_specs, check_vma=False)
```

```python
import functools
import math

import jax
import jax.numpy as jnp
import numpy as np
from jax import lax
from jax.experimental import pallas as pl
from jax.experimental.pallas import tpu as pltpu
from jax.sharding import PartitionSpec as P

C = 192
HEADS = 6
HEAD = 32
FF = 768
Z = 8
WZ = 2
WLAT = 6
WLON = 12
HLAT = 3
HLON = 6
SPAN = WZ * WLAT * WLON
QB = WZ * HLAT * HLON
QUAD = Z * HLAT * HLON
BAND = 2 * WLON - 1
TROW = WLAT * BAND
TW = 384
TILES = TW // 128
QP = 40
SP = 4 * QP
QL = HEADS * QP
PEN = 300
ONE = 330
TSPAN = 168

EPS = 1e-05
LOG2E = math.log2(math.e)
BIG = -1e30
F32 = jnp.float32
BF16 = jnp.bfloat16
NT = (((1,), (1,)), ((), ()))


def key_select(masked):
    sel = np.zeros((TW, SP), np.float32)
    for part in range(4):
        for zj in range(WZ):
            for r in range(HLAT):
                for o in range(HLON):
                    col = part * QP + zj * 18 + r * 6 + o
                    rj = part // 2 * HLAT + r
                    oj = part % 2 * HLON + o
                    sel[zj * TROW + rj * BAND + oj + WLON - 1, col] = 1
                    if masked:
                        sel[PEN + zj, col] = 1
                        sel[PEN + 2 + part // 2, col] = 1
        sel[ONE : ONE + WLON, part * QP + QB : (part + 1) * QP] = BIG
    return sel


def normalize(values, gain):
    mean = jnp.mean(values, axis=-1, keepdims=True)
    centered = values - mean
    var = jnp.mean(centered * centered, axis=-1, keepdims=True)
    return (centered * lax.rsqrt(var + EPS) * gain).astype(BF16)


def dot(a, b):
    return jnp.dot(a, b, preferred_element_type=F32)


def dot_nt(a, b):
    return lax.dot_general(a, b, NT, preferred_element_type=F32)


def table_rows(table, half, rows_ref):
    blank = jnp.zeros((HEADS, TW - 2 * TROW), F32)
    lane = lax.broadcasted_iota(jnp.int32, blank.shape, 1) + 2 * TROW
    blank = jnp.where(lane == ONE, 1.0, blank)
    for zi in range(WZ):
        for r in range(HLAT):
            at = [((zi * WZ + zj) * WLAT + half * HLAT + r) * TROW for zj in range(WZ)]
            wide = jnp.concatenate([table[:, k : k + TROW] for k in at] + [blank], axis=1)
            for t in range(TILES):
                rows_ref[t, pl.ds(zi * HLAT + r, HEADS, stride=8), :] = (
                    wide[:, t * 128 : (t + 1) * 128]
                )


def joined(tiles):
    return jnp.concatenate([tiles[t] for t in range(TILES)], axis=-1)


def expand_rows(rows, first, chunk, wide_ref):
    for o in range(HLON):
        shift = first + o
        rolled = pltpu.roll(rows, shift, 1) if shift else rows
        for h in range(HEADS):
            for t in range(TILES):
                wide_ref[chunk, t, pl.ds(h * QP + o, 6, stride=6), :] = (
                    rolled[h * 8 : h * 8 + 6, t * 128 : (t + 1) * 128]
                )


def head_lanes():
    lanes = lax.broadcasted_iota(jnp.int32, (1, C), 1)
    return [(lanes >= h * HEAD) & (lanes < (h + 1) * HEAD) for h in range(HEADS)]


def attend(items):
    own = head_lanes()
    stacks = [
        jnp.concatenate([jnp.where(own[h], q, 0.0) for h in range(HEADS)], axis=0).astype(BF16)
        for _, _, q, _ in items
    ]
    scores = [dot_nt(st, it[0]) + it[3]() for st, it in zip(stacks, items)]
    weights = [
        jnp.exp2(s - jnp.max(s, axis=1, keepdims=True)).astype(BF16) for s in scores
    ]
    mixed = [dot(p, it[1]) for p, it in zip(weights, items)]
    outs = []
    for m in mixed:
        scaled = m[:, :C] * (1.0 / m[:, C : C + 1])
        out = scaled[:QP]
        for h in range(1, HEADS):
            out = jnp.where(own[h], scaled[h * QP : (h + 1) * QP], out)
        outs.append(out)
    return outs


class Fetch:
    def __init__(self, sems):
        self.sems = sems
        self.copies = {}

    def start(self, name, source, target):
        copy = pltpu.make_async_copy(source, target, self.sems.at[len(self.copies)])
        self.copies[name] = copy
        copy.start()

    def wait(self, *names):
        for name in names:
            self.copies[name].wait()


def feed_forward(resid, mixed, gain_two, w_proj, w_up, w_down_t):
    first = (resid + dot(mixed, w_proj)).astype(BF16)
    first32 = first.astype(F32)
    inner = normalize(first32, gain_two)
    hidden = dot(inner, w_up)
    hidden = (hidden * 0.5 * (1.0 + lax.erf(hidden * (0.5**0.5)))).astype(BF16)
    return first32 + dot_nt(hidden, w_down_t)


QSCALE = HEAD**-0.5 * LOG2E


def with_ones(values):
    lanes = lax.broadcasted_iota(jnp.int32, values.shape, 1)
    return jnp.where(lanes == C, 1.0, values).astype(BF16)


def value_weights(qkv_ref):
    return jnp.concatenate([qkv_ref[:, 2 * C :], jnp.zeros((C, 256 - C), BF16)], axis=1)


def tiles_of(value):
    return value[:, :128], jnp.concatenate([value[:, 128:], value[:, 128:]], axis=1)


def whole_row(first, second):
    return jnp.concatenate([first, second[:, : C - 128]], axis=1)


def first_kernel(
    x_ref, gains_ref, wqkv_ref, wproj_ref, wup_ref, wdown_ref, tab_ref,
    select_ref,
    fast_ref, slow_ref,
    plain_ref, tok_ref, o_ref, rows_ref, wide_ref,
):
    plain_ref[...] = jnp.zeros_like(plain_ref)
    for r in range(WLAT):
        for o in range(WLON):
            part = r // HLAT * 2 + o // HLON
            at = (r % HLAT) * 6 + o % HLON
            for t, tile in enumerate(tiles_of(x_ref[r, o].astype(F32))):
                plain_ref[part, t, pl.ds(at, Z, stride=18), :] = tile
    for part in range(4):
        for w in range(4):
            rows = pl.ds(w * QB, QP)
            at = (part * 4 + w) * QP
            tok_ref[at : at + QP, :] = whole_row(plain_ref[part, 0, rows, :], plain_ref[part, 1, rows, :])
    select = select_ref[...].astype(BF16)
    for w in range(4):
        table = tab_ref[0, w, :, 0, :] * LOG2E
        for a in range(2):
            table_rows(table, a, rows_ref.at[a])
            rows = joined(rows_ref.at[a])
            for b in range(2):
                expand_rows(rows, b * HLON, w * 4 + a * 2 + b, wide_ref)
    gain_one = gains_ref[0, 0:1]
    gain_two = gains_ref[0, 1:2]
    wqk = wqkv_ref[0, :, : 2 * C]
    wv = value_weights(wqkv_ref.at[0])
    for w in range(4):
        tokens = jnp.concatenate(
            [tok_ref[(part * 4 + w) * QP : (part * 4 + w + 1) * QP, :] for part in range(4)], axis=0
        )
        normed = normalize(tokens, gain_one)
        both = dot(normed, wqk)
        query = both[:, :C] * QSCALE
        keys = both[:, C:].astype(BF16)
        values = with_ones(dot(normed, wv))
        items = [
            (keys, values, query[part * QP : (part + 1) * QP],
             lambda chunk=w * 4 + part: dot(joined(wide_ref.at[chunk]).astype(BF16), select))
            for part in range(4)
        ]
        for part, out in enumerate(attend(items)):
            o_ref[(part * 4 + w) * QP : (part * 4 + w + 1) * QP, :] = out
    tok_ref[...] = feed_forward(
        tok_ref[...], o_ref[...].astype(BF16), gain_two, wproj_ref[0], wup_ref[0], wdown_ref[0]
    )
    for part in range(4):
        for w in range(4):
            at = (part * 4 + w) * QP
            for t, tile in enumerate(tiles_of(tok_ref[at : at + QB, :])):
                plain_ref[part, t, pl.ds(w * QB, QB), :] = tile
                if w == 0:
                    plain_ref[part, t, pl.ds(QUAD, 18), :] = tile[:18]
    even = lax.axis_index("lon") % 2 == 0
    low = lax.broadcasted_iota(jnp.int32, (QP, 128), 1) < 128 - (C - 128)
    for a in range(2):
        for pair in range(2):
            rows = [pl.ds((pair * 2 + k) * QB + 18, QP) for k in range(2)]
            sides = []
            for b in range(2):
                part = a * 2 + b
                lasts = [plain_ref[part, 1, r, :] for r in rows]
                sides.append([plain_ref[part, 0, r, :] for r in rows] + [jnp.where(low, lasts[0], lasts[1])])
            for k, (left, right) in enumerate(zip(*sides)):
                fast_ref[a, pair * 3 + k] = jnp.where(even, right, left).astype(BF16)
                slow_ref[a, pair * 3 + k] = jnp.where(even, left, right).astype(BF16)


def block_of(tiles_ref, zw):
    pair, second = divmod(zw, 2)
    last = tiles_ref[pair * 3 + 2].astype(F32)
    if second:
        last = pltpu.roll(last, 64, 1)
    return whole_row(tiles_ref[pair * 3 + second].astype(F32), last)


def bias_kernel(tab_ref, prev_tab_ref, select_ref, bias_ref, rows_ref, work_ref, tv_ref, sems):
    fetch = Fetch(sems)
    fetch.start("own", tab_ref.at[1], tv_ref.at[1])
    fetch.start("prev", prev_tab_ref.at[1], tv_ref.at[0])
    fetch.wait("own", "prev")
    select = select_ref[...].astype(BF16)
    lane = lax.broadcasted_iota(jnp.int32, (QL, 128), 1) + 256
    zi = (lax.broadcasted_iota(jnp.int32, (QL, 1), 0) % QP) // 18
    pen_z = jnp.where(((lane == PEN) & (zi == 1)) | ((lane == PEN + 1) & (zi == 0)), BIG, 0.0)
    lane_row = lane[:1]
    pens = (
        jnp.where((lane_row == PEN + 2) & (lax.axis_index("lat") == 0), BIG, 0.0),
        jnp.where((lane_row == PEN + 3) & (lax.axis_index("lat") == lax.axis_size("lat") - 1), BIG, 0.0),
    )
    for zw in range(4):
        for a in range(2):
            table_rows(tv_ref[a, zw, :, 0, :] * LOG2E, 1 - a, rows_ref.at[a])
            rows = joined(rows_ref.at[a])
            for b in range(2):
                slot = (zw % 2) * 4 + b * 2 + a
                expand_rows(rows, (1 - b) * HLON, slot, work_ref)
                tail = work_ref[slot, 2] + pens[a]
                if zw == 3:
                    tail = tail + pen_z
                wide = jnp.concatenate([work_ref[slot, 0], work_ref[slot, 1], tail], axis=1)
                bias_ref[(b * 2 + a) * 4 + zw] = dot(wide.astype(BF16), select).astype(BF16)


def holed(value, axis):
    blank = jnp.zeros((value.shape[0], 64) if axis else (64, value.shape[1]), value.dtype)
    head, last = (value[:, :128], value[:, 128:]) if axis else (value[:128], value[128:])
    return (
        jnp.concatenate([head, last, blank], axis=axis),
        jnp.concatenate([head, blank, last], axis=axis),
    )


def holed_normalize(sources, zw, gain):
    pair, second = divmod(zw, 2)
    values = jnp.concatenate(
        [
            jnp.concatenate([src[pair * 3 + second], src[pair * 3 + 2]], axis=1).astype(F32)
            for src in sources
        ],
        axis=0,
    )
    lanes = lax.broadcasted_iota(jnp.int32, (1, 256), 1)
    there = (lanes < 128) | (lanes >= 192) if second else lanes < C
    mean = jnp.sum(jnp.where(there, values, 0.0), axis=-1, keepdims=True) * (1.0 / C)
    centered = jnp.where(there, values - mean, 0.0)
    var = jnp.sum(centered * centered, axis=-1, keepdims=True) * (1.0 / C)
    return (centered * lax.rsqrt(var + EPS) * gain).astype(BF16)


def second_kernel(
    fast_any, slow_any, from_fast_any, from_slow_any, lat_fast_any, lat_slow_any, bias_any,
    gains_ref, wqkv_any, wproj_any, wup_any, wdown_any,
    out_ref,
    plain_ref, own_ref, o_ref,
    near_ref, vert_ref, bias_ref,
    qkv_ref, proj_ref, up_ref, down_ref, sems,
):
    fetch = Fetch(sems)
    even = 1 - lax.axis_index("lon") % 2
    lat_even = 1 - lax.axis_index("lat") % 2
    columns = (1 + even, 2 - even, 3 * even, 3 - 3 * even)
    sides = (fast_any, slow_any, from_fast_any, from_slow_any)
    for i in range(2):
        fetch.start(f"near{i}", sides[i], near_ref.at[columns[i]])
    fetch.start("qkv", wqkv_any.at[1], qkv_ref)
    for i in range(2, 4):
        fetch.start(f"near{i}", sides[i], near_ref.at[columns[i]])
    for i in range(4):
        fetch.start(f"fast{i}", lat_fast_any.at[i], vert_ref.at[lat_even, columns[i]])
        fetch.start(f"slow{i}", lat_slow_any.at[i], vert_ref.at[1 - lat_even, columns[i]])
    fetch.start("bias", bias_any, bias_ref)
    fetch.start("proj", wproj_any.at[1], proj_ref)
    fetch.start("up", wup_any.at[1], up_ref)
    fetch.start("down", wdown_any.at[1], down_ref)
    gain_one = gains_ref[1, 0:1]
    gain_two = gains_ref[1, 1:2]
    fetch.wait("near0", "near1", "qkv")
    wq = qkv_ref[:, :C]
    wk = holed(qkv_ref[:, C : 2 * C], 0)
    wv = holed(value_weights(qkv_ref), 0)
    gains = holed(gain_one, 1)
    for b in range(2):
        for a in range(2):
            for zw in range(4):
                at = ((b * 2 + a) * 4 + zw) * QP
                own_ref[at : at + QP, :] = block_of(near_ref.at[1 + b, a], zw)
    query = dot(normalize(own_ref[...], gain_one), wq) * QSCALE
    fetch.wait("near2", "near3")
    fetch.wait(*[f"{kind}{i}" for kind in ("fast", "slow") for i in range(4)])
    above = [vert_ref.at[0, i] for i in range(4)]
    here = [[near_ref.at[i, a] for i in range(4)] for a in range(2)]
    below = [vert_ref.at[1, i] for i in range(4)]
    for b in range(2):
        for a in range(2):
            pair = (above, here[0]) if a == 0 else (here[1], below)
            sources = [pair[part // 2][b * 2 + part % 2] for part in range(4)]
            items = []
            for zw in range(4):
                chunk = (b * 2 + a) * 4 + zw
                normed = holed_normalize(sources, zw, gains[zw % 2])
                keys = dot(normed, wk[zw % 2]).astype(BF16)
                values = with_ones(dot(normed, wv[zw % 2]))
                items.append(
                    (keys, values, query[chunk * QP : (chunk + 1) * QP],
                     lambda chunk=chunk: bias_ref[chunk].astype(F32))
                )
            if a == b == 0:
                fetch.wait("bias")
            for zw, out in enumerate(attend(items)):
                chunk = (b * 2 + a) * 4 + zw
                o_ref[chunk * QP : (chunk + 1) * QP, :] = out
    fetch.wait("proj", "up", "down")
    own_ref[...] = feed_forward(
        own_ref[...], o_ref[...].astype(BF16), gain_two, proj_ref[...], up_ref[...], down_ref[...]
    )
    for part in range(4):
        a, b = divmod(part, 2)
        for zw in range(4):
            at = ((b * 2 + a) * 4 + zw) * QP
            for t, tile in enumerate(tiles_of(own_ref[at : at + QB, :])):
                if zw < 3:
                    plain_ref[part, t, pl.ds(zw * QB + 18, QB), :] = tile
                else:
                    plain_ref[part, t, pl.ds(zw * QB + 18, 18), :] = tile[:18]
                    plain_ref[part, t, pl.ds(0, 18), :] = tile[18:]
    for r in range(WLAT):
        for o in range(WLON):
            part = r // HLAT * 2 + o // HLON
            at = (r % HLAT) * 6 + o % HLON
            out_ref[r, o] = whole_row(
                plain_ref[part, 0, pl.ds(at, Z, stride=18), :], plain_ref[part, 1, pl.ds(at, Z, stride=18), :]
            ).astype(BF16)


def whole(shape):
    return pl.BlockSpec(shape, lambda *_: (0,) * len(shape))


ANY = pl.BlockSpec(memory_space=pl.ANY)


def picked(shape, layer):
    return pl.BlockSpec((1,) + shape[1:], lambda *_: (layer,) + (0,) * (len(shape) - 1))


def weight_specs(layer, gains, w_qkv, w_proj, w_up, w_down):
    return [whole(gains.shape)] + [picked(w.shape, layer) for w in (w_qkv, w_proj, w_up, w_down)]


PARAMS = pltpu.CompilerParams(vmem_limit_bytes=56 * 1024 * 1024)


def shifted(value, axis, steps):
    count = lax.axis_size(axis)
    pairs = [(source, (source + steps) % count) for source in range(count)]
    return lax.ppermute(value, axis, pairs)


def paired(axis, first):
    count = lax.axis_size(axis)
    return [(i, (i + 1 if (i + first) % 2 == 0 else i - 1) % count) for i in range(count)]


def call(kernel, name, in_specs, outs, scratch, args):
    single = not isinstance(outs, list)
    specs = [whole(o.shape) for o in (outs if not single else [outs])]
    return pl.pallas_call(
        kernel,
        grid=(1,),
        in_specs=in_specs,
        out_specs=specs[0] if single else specs,
        out_shape=outs,
        scratch_shapes=scratch,
        compiler_params=PARAMS,
        name=name,
    )(*args)


def shards(grid, gains, w_qkv, w_proj, w_up, w_down, tables):
    grid = grid.transpose(1, 2, 0, 3)
    w_down = w_down.transpose(0, 2, 1)
    tables = tables.transpose(0, 1, 3, 2, 4)
    prev_tables = shifted(tables, "lat", 1)
    plain = jnp.asarray(key_select(False))
    masked = jnp.asarray(key_select(True))
    weights = (gains, w_qkv, w_proj, w_up, w_down)
    half = jax.ShapeDtypeStruct((2, 6, QP, 128), BF16)
    tok = pltpu.VMEM((16 * QP, C), F32)
    plain_tok = pltpu.VMEM((4, 2, TSPAN, 128), F32)
    table_work = pltpu.VMEM((2, TILES, 48, 128), F32)
    weight_mem = [pltpu.VMEM(w.shape[1:], BF16) for w in weights[1:]]
    fast, slow = call(
        first_kernel, "first_layer",
        [whole(grid.shape)] + weight_specs(0, *weights) + [picked(tables.shape, 0), whole(plain.shape)],
        [half, half],
        [plain_tok, tok, tok, table_work, pltpu.VMEM((16, TILES, QL, 128), F32)],
        (grid, *weights, tables, plain),
    )
    from_fast = lax.ppermute(fast, "lon", paired("lon", 0))
    from_slow = lax.ppermute(slow, "lon", paired("lon", 1))
    from_fast, from_slow, prev_tables = lax.optimization_barrier((from_fast, from_slow, prev_tables))
    bias = call(
        bias_kernel, "second_bias",
        [ANY, ANY, whole(masked.shape)],
        jax.ShapeDtypeStruct((16, QL, SP), BF16),
        [table_work, pltpu.VMEM((8, TILES, QL, 128), F32),
         pltpu.VMEM((2,) + tables.shape[1:], F32), pltpu.SemaphoreType.DMA((2,))],
        (tables, prev_tables, masked),
    )
    odd = lax.axis_index("lat") % 2
    sides = (fast, slow, from_fast, from_slow)
    toward_fast = jnp.concatenate([lax.dynamic_slice_in_dim(v, 1 - odd, 1, 0) for v in sides])
    toward_slow = jnp.concatenate([lax.dynamic_slice_in_dim(v, odd, 1, 0) for v in sides])
    lat_fast = lax.ppermute(toward_fast, "lat", paired("lat", 0))
    lat_slow = lax.ppermute(toward_slow, "lat", paired("lat", 1))
    moved = (*sides, lat_fast, lat_slow, bias)
    out = call(
        second_kernel, "second_layer",
        [ANY] * 7 + [whole(gains.shape)] + [ANY] * 4,
        jax.ShapeDtypeStruct(grid.shape, BF16),
        [plain_tok, tok, tok]
        + [pltpu.VMEM((4,) + half.shape, BF16), pltpu.VMEM((2, 4) + half.shape[1:], BF16), pltpu.VMEM(bias.shape, BF16)]
        + weight_mem + [pltpu.SemaphoreType.DMA((17,))],
        (*moved, *weights),
    )
    return out.transpose(2, 0, 1, 3)


def solution(mesh):
    in_specs = (
        P(None, "lat", "lon", None),
        P(),
        P(),
        P(),
        P(),
        P(),
        P(None, None, "lat", None, None),
    )
    out_specs = P(None, "lat", "lon", None)
    return jax.shard_map(shards, mesh=mesh, in_specs=in_specs, out_specs=out_specs, check_vma=False)
```
